128 devices in a mesh: dp: 4 (over x), expert: 32 (over z, y, core).
Axes of the slice: x: 4, y: 4, z: 4, core: 2. Of those that a mesh axis runs over, the one named last changes fastest.
Arguments:
- expert_ids: int32 [4, 4096, 2], P('dp', 'expert'), may hold values from 0 to 7, all different within a row; in each aligned block of 128 rows (0 to 127, 128 to 255, ..., all dimensions but the last counted through in order) at most 34 rows name the same one
- hidden_grad: bfloat16 [4352, 98304], P(None, ('dp', 'expert')), may hold values from -0.1796875 to 0.1796875
- up_weight: bfloat16 [4096, 98304], P(None, ('dp', 'expert')), may hold values from -2.390625 to 2.390625
Outputs:
- token_grad: bfloat16 [4, 4096, 4096], P('dp', 'expert')
The draws below stay inside these ranges and needn't reach their ends.
Inputs may be any that keep to these rules, and one draw needn't show every extreme that they name: `expert_ids`: each token names 2 different experts; among the 128 tokens of one sequence shard no expert is named more than 34 times.
All inputs are finite; a program needn't handle non-finite values.
Results may differ from the reference program's by a relative error of at most 0.018.
Values may be sent and summed in bfloat16 or wider, within the bound.
A program may use at most 256 MiB of HBM per device.

```python
import math
import jax
import jax.numpy as jnp
import numpy as np
from jax import lax

D = 4096
EXPERTS = 8
TOPK = 2
TOK_DEV = 128
SPLIT = 4
HID_DEV = 768
SEND = 34
ROWS = 1088
SEQ = 4096
N_DP = 4
N_EXPERT = 32
DEVICES = 128


def steps_of(key, extent, cuts, smallest, high):
    def one(axis_at, shards_of):
        heights = jax.random.uniform(jax.random.fold_in(jax.random.fold_in(key, 6), axis_at), (shards_of,), jnp.float32, smallest / len(cuts), high / len(cuts))
        return jnp.repeat(jnp.exp(heights), extent[axis_at] // shards_of).reshape((-1,) + (1,) * (len(extent) - axis_at - 1))

    factor_of = one(*cuts[0])
    for cut in cuts[1:]:
        factor_of = factor_of * one(*cut)
    return factor_of


def deal_out(rng, own, number, rows, amount, top, bound, lean):
    order = jax.random.permutation(rng, amount)
    heavy_load, ordinary = load_shares(amount, rows * top, bound, lean, True), load_shares(amount, rows * top, bound, lean, False)
    places = jnp.arange(amount)

    def named(sizes, offset_by):
        used = int((sizes > 0).sum())
        fixed = max(1, used // 4)
        shifted = fixed + (places - fixed + offset_by * (used - fixed)) % max(1, amount - fixed)
        return jnp.zeros((amount,), jnp.int32).at[order[jnp.where(places < fixed, places, shifted)]].set(jnp.asarray(sizes, jnp.int32))

    sizes = jnp.where(number % 4 == 0, named(heavy_load, number // 4), named(ordinary, number - number // 4 - 1))
    mixed = jax.random.permutation(jax.random.fold_in(own, 3), amount)
    source_of, taker = mixed[0:amount // 2 * 2:2], mixed[1:amount // 2 * 2:2]
    margin = jnp.minimum(sizes[source_of] - 1, bound - sizes[taker]) // 2
    margin = jnp.where((source_of == order[0]) | (taker == order[0]) | (sizes[taker] == 0), 0, jnp.maximum(margin, 0))
    shifted = jax.random.randint(jax.random.fold_in(own, 4), (amount // 2,), 0, 1 << 20) % (margin + 1)
    sizes = sizes.at[source_of].add(-shifted).at[taker].add(shifted)
    members = jnp.searchsorted(jnp.cumsum(sizes), jnp.arange(rows * top), side="right").astype(jnp.int32)
    listing = members.reshape(top, rows).T
    listing = listing[jax.random.permutation(jax.random.fold_in(own, 1), rows)]
    offset_by = jax.random.randint(jax.random.fold_in(own, 2), (rows, 1), 0, top)
    return jnp.take_along_axis(listing, (jnp.arange(top)[None, :] + offset_by) % top, axis=1)


def load_shares(amount, total, most, lean, full):
    weights = [(1 << 20) // math.isqrt(rank ** lean) + 1 for rank in range(1, amount + 1)]
    largest = most if full else min(most, max(-(-total // amount), total * weights[0] // sum(weights)))
    least = 1 if total - largest >= amount - 1 else 0
    given, surplus = [largest] + [least] * (amount - 1), total - largest - least * (amount - 1)
    while surplus > 0:
        movable = [i for i in range(1, amount) if given[i] < largest] or [i for i in range(1, amount) if given[i] < most]
        mass, left = sum([weights[i] for i in movable]), surplus
        for i in movable:
            addition = min(most - given[i], max(1, left * weights[i] // mass), surplus)
            given[i] = given[i] + addition
            surplus = surplus - addition
    return np.array(given)


def normal_values(stream_key, extent, scale, reach, shards=(), held_as=jnp.bfloat16):
    entries = scale * jax.random.normal(stream_key, extent, jnp.float32)
    if shards:
        entries = entries * steps_of(stream_key, extent, shards, -0.22, 0.18)
    return jnp.clip(entries, -reach, reach).astype(held_as)


def setup_inputs(seed: int = 0) -> dict:
    seeds = jax.random.split(jax.random.key(seed), 4)
    expert_ids_keys = jax.random.split(jax.random.fold_in(seeds[0], 1), N_DP * SEQ // TOK_DEV)
    expert_ids_turns = jax.random.permutation(jax.random.fold_in(seeds[0], 3), N_DP * SEQ // TOK_DEV)
    expert_ids = jax.vmap(lambda own, number: deal_out(jax.random.fold_in(seeds[0], 2), own, number, TOK_DEV, EXPERTS, TOPK, SEND, 2))(expert_ids_keys, expert_ids_turns).reshape((N_DP, SEQ, TOPK))
    hidden_grad = normal_values(seeds[1], (N_DP * ROWS, HID_DEV * DEVICES), 0.03, 0.1796875, ((1, 128),))
    up_weight = normal_values(seeds[2], (D, HID_DEV * DEVICES), 0.4, 2.390625, ((1, 128),))
    return {"expert_ids": expert_ids, "hidden_grad": hidden_grad, "up_weight": up_weight}


def reference(expert_ids, hidden_grad, up_weight):
    pair_ids = expert_ids.reshape(N_DP, N_EXPERT, TOK_DEV * TOPK)
    one_hot = (pair_ids[..., None] == jnp.arange(EXPERTS, dtype=jnp.int32)).astype(jnp.int32)
    before = jnp.cumsum(one_hot, axis=2) - one_hot
    slots = jnp.sum(before * one_hot, axis=3).reshape(N_DP, SEQ, TOPK).astype(jnp.int32)
    group_index = jnp.arange(N_DP, dtype=jnp.int32)[:, None, None]
    shard_index = (jnp.arange(SEQ, dtype=jnp.int32) // TOK_DEV)[None, :, None]
    row_index = (group_index * ROWS + shard_index * SEND + slots).astype(jnp.int32)
    grad_blocks = hidden_grad.reshape(N_DP * ROWS, N_DP, N_EXPERT, HID_DEV)
    weight_blocks = up_weight.reshape(D, N_DP, N_EXPERT, HID_DEV)

    def one_column(column):
        grads = lax.dynamic_index_in_dim(grad_blocks, column, 2, keepdims=False)
        weights = lax.dynamic_index_in_dim(weight_blocks, column, 2, keepdims=False)
        partial_value = jnp.einsum("rju,dju->jrd", grads.astype(jnp.float32), weights.astype(jnp.float32)).astype(jnp.bfloat16)
        return jnp.sum(partial_value.astype(jnp.float32), axis=0).astype(jnp.bfloat16)

    row_grads = lax.map(one_column, jnp.arange(N_EXPERT, dtype=jnp.int32))
    column_index = (expert_ids[..., None] * SPLIT + jnp.arange(SPLIT, dtype=jnp.int32)).astype(jnp.int32)
    picked = row_grads[column_index, row_index[..., None]]
    return jnp.sum(picked.astype(jnp.float32), axis=(2, 3)).astype(jnp.bfloat16)
```

```python
import functools

import jax
import jax.numpy as jnp
from jax import lax
from jax.experimental import pallas as pl
from jax.experimental.pallas import tpu as pltpu
from jax.sharding import PartitionSpec as P

EXPERTS = 8
SLOTS = 34
SHARDS = 8
BLOCK = SLOTS * SHARDS
GROUP = 4 * BLOCK
TOKENS = 128
WIDE = 256
HALF = 128
MESH = pl.DeviceIdType.MESH
BF = jnp.bfloat16
F32 = jnp.float32


def nt_dot(a, b):
    return lax.dot_general(a, b, (((1,), (1,)), ((), ())), preferred_element_type=F32)


def kernel(
    chunks, ids_ref, hid_ref, w_ref, out_ref,
    a_buf, w_buf, xs, xr, zb, ys, yr, sel, fin, keys,
    in_sem, core_send, core_recv, key_send, key_recv,
    x_send, x_recv, z_send, z_recv, y_send, y_recv, o_send, o_recv,
):
    x = lax.axis_index("dp")
    col = lax.axis_index("expert")
    z, y, k = col // 8, (col // 2) % 4, col % 2
    half_cols = chunks * WIDE
    hid = hid_ref.shape[1]

    def dev(dx=0, dz=0, dy=0, dk=0):
        return ((x + dx) % 4, ((z + dz) % 4) * 8 + ((y + dy) % 4) * 2 + (k + dk) % 2)

    def rows_of(start, size):
        return pl.ds(pl.multiple_of(start, 16), size)

    def remote(src, dst, send, recv, to):
        return pltpu.make_async_remote_copy(
            src_ref=src, dst_ref=dst, send_sem=send, recv_sem=recv, device_id=to, device_id_type=MESH
        )

    group_order = [(x + 2) % 4, (x + 3) % 4, (x + 1) % 4, x]

    def local_a(i):
        rows = rows_of(group_order[i] * GROUP, GROUP)
        return pltpu.make_async_copy(hid_ref.at[rows], a_buf.at[0, rows], in_sem.at[i])

    def local_w(j):
        return pltpu.make_async_copy(
            w_ref.at[rows_of(k * half_cols + j * WIDE, WIDE)], w_buf.at[0, rows_of(j * WIDE, WIDE)], in_sem.at[4 + j]
        )

    def core_a(i):
        rows = rows_of(group_order[i] * GROUP, GROUP)
        return remote(hid_ref.at[rows], a_buf.at[1, rows], core_send.at[i], core_recv.at[i], dev(dk=1))

    def core_w(j):
        return remote(
            w_ref.at[rows_of((1 - k) * half_cols + j * WIDE, WIDE)],
            w_buf.at[1, rows_of(j * WIDE, WIDE)],
            core_send.at[4 + j], core_recv.at[4 + j], dev(dk=1),
        )

    peers = [(dy, dk) for dy in range(4) for dk in range(2) if (dy, dk) != (0, 0)]

    def key_copy(i):
        dy, dk = peers[i]
        mine = y * 2 + k
        return remote(keys.at[mine], keys.at[mine], key_send.at[i], key_recv.at[i], dev(dy=dy, dk=dk))

    def tree_copy(sends, recvs, s_sem, r_sem, axis, c, kind, side):
        step = 1 if (side == 0) != (kind == 1) else -1
        src = recvs.at[c, 0, side] if kind == 2 else sends.at[c, kind, side]
        return remote(
            src, recvs.at[c, kind, side], s_sem.at[c, kind, side], r_sem.at[c, kind, side], dev(**{axis: step})
        )

    x_copy = functools.partial(tree_copy, xs, xr, x_send, x_recv, "dx")
    y_copy = functools.partial(tree_copy, ys, yr, y_send, y_recv, "dy")

    def z_copy(c, i):
        there = (z + i + 1) % 4
        return remote(
            xr.at[c, 1, :, rows_of(there * BLOCK, BLOCK), :],
            zb.at[c, :, rows_of(z * BLOCK, BLOCK), :],
            z_send.at[c, i], z_recv.at[c, i], dev(dz=i + 1),
        )

    def o_copy(c):
        return remote(
            fin.at[c, rows_of((1 - k) * TOKENS, TOKENS)],
            out_ref.at[:, pl.ds(pl.multiple_of(k * half_cols + c * WIDE, WIDE), WIDE)],
            o_send.at[c], o_recv.at[c], dev(dk=1),
        )

    local_w(0).start()
    for i in range(4):
        local_a(i).start()
    for j in range(1, chunks):
        local_w(j).start()

    barrier = pltpu.get_barrier_semaphore()
    near = [dev(dx=1), dev(dx=3)] + [dev(dz=i) for i in (1, 2, 3)] + [dev(dy=a, dk=b) for a, b in peers]
    for to in near:
        pl.semaphore_signal(barrier, inc=1, device_id=to, device_id_type=MESH)
    pl.semaphore_wait(barrier, len(near))

    core_w(0).start()
    core_a(0).start()
    core_w(1).start()
    for i in range(1, 4):
        core_a(i).start()
    for j in range(2, chunks):
        core_w(j).start()

    ids = ids_ref[...]
    experts = lax.broadcasted_iota(jnp.int32, (EXPERTS, TOKENS), 0)
    ones = [ids[i:i + 1, :] == experts for i in range(2)]
    counts = (ones[0].astype(F32) + ones[1].astype(F32)).astype(BF)
    earlier = lax.broadcasted_iota(jnp.int32, (TOKENS, TOKENS), 0) < lax.broadcasted_iota(jnp.int32, (TOKENS, TOKENS), 1)
    before = jnp.dot(counts, earlier.astype(F32).astype(BF), preferred_element_type=F32)
    code_rows = []
    for i in range(2):
        position = jnp.sum(jnp.where(ones[i], before, 0.0), axis=0, keepdims=True).astype(jnp.int32)
        if i == 1:
            position = position + (ids[0:1, :] == ids[1:2, :]).astype(jnp.int32)
        expert = ids[i:i + 1, :]
        code_rows.append((expert % 2) * GROUP + (expert // 2) * BLOCK + position)
    row = lax.broadcasted_iota(jnp.int32, (8, TOKENS), 0)
    keys[y * 2 + k] = jnp.where(row == 0, code_rows[0], code_rows[1])
    for i in range(7):
        key_copy(i).start()

    def product(g, c, r):
        rows = rows_of(g * GROUP + r * BLOCK, BLOCK)
        cols = rows_of(c * WIDE, WIDE)
        return nt_dot(a_buf[0, rows, :], w_buf[0, cols, :]) + nt_dot(a_buf[1, rows, :], w_buf[1, cols, :])

    def tiles(body):
        lax.fori_loop(0, 4, lambda r, _: (body(r), 0)[1], 0)

    def wait_a(i):
        local_a(i).wait()
        core_a(i).wait_recv()

    def s0(c):
        local_w(c).wait()
        core_w(c).wait_recv()

        @pl.when(c == 0)
        def _():
            wait_a(0)

        def body(r):
            acc = product((x + 2) % 4, c, r)
            rows = rows_of(r * BLOCK, BLOCK)
            xs[c, 0, 0, rows, :] = acc[:, :HALF].astype(BF)
            xs[c, 0, 1, rows, :] = acc[:, HALF:].astype(BF)

        tiles(body)
        x_copy(c, 0, 0).start()
        x_copy(c, 0, 1).start()

    def s1(c):
        for i, side in ((1, 0), (2, 1)):
            @pl.when(c == 0)
            def _():
                wait_a(i)

            other = 1 - side
            g = (x + 3) % 4 if side == 0 else (x + 1) % 4
            x_copy(c, 0, other).wait_recv()

            def body(r):
                acc = product(g, c, r)
                rows = rows_of(r * BLOCK, BLOCK)
                part = [acc[:, :HALF], acc[:, HALF:]]
                xs[c, 1, side, rows, :] = part[side].astype(BF)
                xr[c, 0, other, rows, :] = (part[other] + xr[c, 0, other, rows, :].astype(F32)).astype(BF)

            tiles(body)
            x_copy(c, 2, other).start()
            x_copy(c, 1, side).start()

    def s2(c):
        @pl.when(c == 0)
        def _():
            wait_a(3)

        for side in range(2):
            x_copy(c, 1, side).wait_recv()
            x_copy(c, 2, side).wait_recv()

        def body(r):
            acc = product(x, c, r)
            rows = rows_of(r * BLOCK, BLOCK)
            for side in range(2):
                part = acc[:, side * HALF:(side + 1) * HALF]
                total = part + (xr[c, 1, side, rows, :].astype(F32) + xr[c, 2, side, rows, :].astype(F32))
                xr[c, 1, side, rows, :] = total.astype(BF)

        tiles(body)
        for i in range(3):
            z_copy(c, i).start()
        mine = rows_of(z * BLOCK, BLOCK)
        zb[c, :, mine, :] = xr[c, 1, :, mine, :]

    def tokens_of(c, yy):
        chosen = sel[rows_of(yy * 2 * TOKENS, 2 * TOKENS), :]
        values = jnp.concatenate([zb[c, 0], zb[c, 1]], axis=1)
        return jnp.dot(chosen, values, preferred_element_type=F32)

    def s3(c):
        @pl.when(c == 0)
        def _():
            for i in range(7):
                key_copy(i).wait_recv()
            lanes = lax.broadcasted_iota(jnp.int32, (TOKENS, GROUP), 1).astype(F32)

            def build(s, _):
                turned = jnp.transpose(keys[s].astype(F32))
                shift = (s * SLOTS - (y // 2) * GROUP).astype(F32)
                hit = (turned[:, 0:1] + shift == lanes) | (turned[:, 1:2] + shift == lanes)
                sel[rows_of(s * TOKENS, TOKENS), :] = hit.astype(F32).astype(BF)
                return 0

            lax.fori_loop(0, SHARDS, build, 0)

        for i in range(3):
            z_copy(c, i).wait_recv()
        acc = tokens_of(c, (y + 2) % 4)
        ys[c, 0, 0] = acc[:, :HALF].astype(BF)
        ys[c, 0, 1] = acc[:, HALF:].astype(BF)
        y_copy(c, 0, 0).start()
        y_copy(c, 0, 1).start()

    def s4(c):
        for side in range(2):
            other = 1 - side
            acc = tokens_of(c, (y + 3) % 4 if side == 0 else (y + 1) % 4)
            part = [acc[:, :HALF], acc[:, HALF:]]
            ys[c, 1, side] = part[side].astype(BF)
            y_copy(c, 1, side).start()
            y_copy(c, 0, other).wait_recv()
            yr[c, 0, other] = (part[other] + yr[c, 0, other].astype(F32)).astype(BF)
            y_copy(c, 2, other).start()

    def s5(c):
        acc = tokens_of(c, y)
        for side in range(2):
            y_copy(c, 1, side).wait_recv()
            y_copy(c, 2, side).wait_recv()
            part = acc[:, side * HALF:(side + 1) * HALF]
            total = part + (yr[c, 1, side].astype(F32) + yr[c, 2, side].astype(F32))
            fin[c, :, side * HALF:(side + 1) * HALF] = total.astype(BF)
        o_copy(c).start()
        cols = pl.ds(pl.multiple_of(k * half_cols + c * WIDE, WIDE), WIDE)
        out_ref[:, cols] = fin[c, rows_of(k * TOKENS, TOKENS), :]

    def step(i, _):
        for lag, stage in ((0, s0), (1, s1), (3, s3), (4, s4), (5, s5), (2, s2)):
            @pl.when((i >= lag) & (i - lag < chunks))
            def _():
                stage(i - lag)
        return 0

    lax.fori_loop(0, chunks + 5, step, 0)

    def finish(c, _):
        core_w(c).wait_send()
        for kind in range(3):
            for side in range(2):
                x_copy(c, kind, side).wait_send()
                y_copy(c, kind, side).wait_send()
        for i in range(3):
            z_copy(c, i).wait_send()
        o_copy(c).wait()
        return 0

    lax.fori_loop(0, chunks, finish, 0)
    for i in range(4):
        core_a(i).wait_send()
    for i in range(7):
        key_copy(i).wait_send()


def on_device(expert_ids, hidden_grad, up_weight):
    rows, hid = hidden_grad.shape
    width = up_weight.shape[0]
    chunks = width // 2 // WIDE
    dma = pltpu.SemaphoreType.DMA
    out = pl.pallas_call(
        functools.partial(kernel, chunks),
        out_shape=jax.ShapeDtypeStruct((TOKENS, width), BF),
        in_specs=[
            pl.BlockSpec(memory_space=pltpu.VMEM),
            pl.BlockSpec(memory_space=pl.ANY),
            pl.BlockSpec(memory_space=pl.ANY),
        ],
        out_specs=pl.BlockSpec(memory_space=pltpu.VMEM),
        scratch_shapes=[
            pltpu.VMEM((2, rows, hid), BF),
            pltpu.VMEM((2, width // 2, hid), BF),
            pltpu.VMEM((chunks, 2, 2, GROUP, HALF), BF),
            pltpu.VMEM((chunks, 3, 2, GROUP, HALF), BF),
            pltpu.VMEM((chunks, 2, GROUP, HALF), BF),
            pltpu.VMEM((chunks, 2, 2, 2 * TOKENS, HALF), BF),
            pltpu.VMEM((chunks, 3, 2, 2 * TOKENS, HALF), BF),
            pltpu.VMEM((SHARDS * TOKENS, GROUP), BF),
            pltpu.VMEM((chunks, 2 * TOKENS, WIDE), BF),
            pltpu.VMEM((SHARDS, 8, TOKENS), jnp.int32),
            dma((4 + chunks,)), dma((4 + chunks,)), dma((4 + chunks,)),
            dma((7,)), dma((7,)),
            dma((chunks, 3, 2)), dma((chunks, 3, 2)),
            dma((chunks, 3)), dma((chunks, 3)),
            dma((chunks, 3, 2)), dma((chunks, 3, 2)),
            dma((chunks,)), dma((chunks,)),
        ],
        compiler_params=pltpu.CompilerParams(
            collective_id=0, has_side_effects=True, vmem_limit_bytes=63 * 2**20
        ),
        cost_estimate=pl.CostEstimate(
            flops=2 * rows * hid * width, bytes_accessed=2 * (rows + width) * hid + 2 * TOKENS * width, transcendentals=0
        ),
        name="up_cotangent",
    )(expert_ids[0].T, hidden_grad, up_weight)
    return out[None]


def solution(mesh):
    return jax.shard_map(
        on_device,
        mesh=mesh,
        in_specs=(P("dp", "expert", None), P(None, ("dp", "expert")), P(None, ("dp", "expert"))),
        out_specs=P("dp", "expert", None),
        check_vma=False,
    )
```

```python
import functools

import jax
import jax.numpy as jnp
from jax import lax
from jax.experimental import pallas as pl
from jax.experimental.pallas import tpu as pltpu
from jax.sharding import PartitionSpec as P

EXPERTS = 8
SLOTS = 34
SHARDS = 8
BLOCK = SLOTS * SHARDS
GROUP = 4 * BLOCK
WINDOW = 80
DEPTH = 4 * WINDOW
TOKENS = 128
WIDE = 256
HALF = 128
MESH = pl.DeviceIdType.MESH
BF = jnp.bfloat16
F32 = jnp.float32


def nt_dot(a, b):
    return lax.dot_general(a, b, (((1,), (1,)), ((), ())), preferred_element_type=F32)


def kernel(
    direct, early, ids_ref, hid_ref, w_ref, out_ref,
    a_buf, w_buf, xs, xr, zb, ys, yr, zs2, zb2, ys2, yr2, ye2, xr2, sel, fin, keys,
    in_sem, core_send, core_recv, key_sem, xt_send, xp_send, xc_send, xt_recv, x_recv,
    z_send, z_recv, y_send, yt_recv, y_recv, z2_send, z2_recv, y2_send, y2t_recv, y2_recv, x2_send, x2t_recv, x2_recv, o_sem,
):
    x = lax.axis_index("dp")
    col = lax.axis_index("expert")
    z, y, k = col // 8, (col // 2) % 4, col % 2
    chunks = direct + early
    half_cols = chunks * WIDE
    slots_x = xs.shape[0]
    slots_z = zs2.shape[0]

    def dev(dx=0, dz=0, dy=0, dk=0):
        return ((x + dx) % 4, ((z + dz) % 4) * 8 + ((y + dy) % 4) * 2 + (k + dk) % 2)

    def rows_of(start, size):
        return pl.ds(pl.multiple_of(start, 16), size)

    def remote(src, dst, send, recv, to):
        return pltpu.make_async_remote_copy(
            src_ref=src, dst_ref=dst, send_sem=send, recv_sem=recv, device_id=to, device_id_type=MESH
        )

    def loop(count, body):
        lax.fori_loop(0, count, lambda i, _: (body(i), 0)[1], 0)

    def nth_group(i):
        return (x + jnp.where(i < 2, i + 2, 3 - i)) % 4

    def local_a(i):
        rows = rows_of(nth_group(i) * GROUP, GROUP)
        return pltpu.make_async_copy(hid_ref.at[rows], a_buf.at[0, rows], in_sem.at[i])

    def local_w(j):
        return pltpu.make_async_copy(
            w_ref.at[rows_of(k * half_cols + j * WIDE, WIDE)], w_buf.at[0, rows_of(j * WIDE, WIDE)], in_sem.at[4 + j]
        )

    def core_a(i):
        rows = rows_of(nth_group(i) * GROUP, GROUP)
        return remote(hid_ref.at[rows], a_buf.at[1, rows], core_send.at[0], core_recv.at[i], dev(dk=1))

    def core_w(j):
        return remote(
            w_ref.at[rows_of((1 - k) * half_cols + j * WIDE, WIDE)],
            w_buf.at[1, rows_of(j * WIDE, WIDE)],
            core_send.at[1], core_recv.at[4 + j], dev(dk=1),
        )

    peers = [(dy, dk) for dy in range(4) for dk in range(2) if (dy, dk) != (0, 0)]

    def key_copy(i):
        dy, dk = peers[i]
        mine = y * 2 + k
        return remote(keys.at[x, mine], keys.at[x, mine], key_sem.at[0], key_sem.at[1], dev(dy=dy, dk=dk))

    def group_copy(i):
        return remote(keys.at[x], keys.at[x], key_sem.at[2], key_sem.at[3], dev(dx=i + 1))

    def wait_bytes(ref, sem):
        pltpu.make_async_copy(ref, ref, sem).wait()

    def tree_copy(source, recvs, s_sems, t_sem, r_sem, axis, c, kind, side):
        step = 1 if (side == 0) != (kind == 1) else -1
        src = recvs.at[c, 0, side] if kind == 2 else source(c, kind, side, step)
        return remote(
            src, recvs.at[c, kind, side], s_sems[kind].at[c],
            t_sem.at[c, side] if kind == 0 else r_sem.at[c], dev(**{axis: step}),
        )

    x_copy = functools.partial(
        tree_copy, lambda c, kind, side, step: xs.at[c % slots_x, kind, side], xr,
        (xt_send, xp_send, xc_send), xt_recv, x_recv, "dx",
    )
    y_copy = functools.partial(
        tree_copy, lambda c, kind, side, step: ys.at[c, kind, side], yr, (y_send,) * 3, yt_recv, y_recv, "dy"
    )
    y2_copy = functools.partial(
        tree_copy, lambda c, kind, side, step: ys2.at[c, kind, side], yr2, (y2_send,) * 3, y2t_recv, y2_recv, "dy"
    )
    x2_copy = functools.partial(
        tree_copy, lambda c, kind, side, step: ye2.at[c, (x + (step if kind else 2)) % 4, side], xr2,
        (x2_send,) * 3, x2t_recv, x2_recv, "dx",
    )

    def wait_through(recvs, t_sem, c, side):
        wait_bytes(recvs.at[c, 0, side], t_sem.at[c, side])

    def wait_tree(recvs, r_sem, c):
        wait_bytes(recvs.at[c, pl.ds(1, 2)], r_sem.at[c])

    def z_copy(c, i):
        there = (z + i + 1) % 4
        return remote(
            xr.at[c, 1, :, rows_of(there * BLOCK, BLOCK), :], zb.at[c, z], z_send.at[c], z_recv.at[c], dev(dz=i + 1)
        )

    def z2_copy(c, g, dz):
        there = rows_of(((z + dz) % 4) * BLOCK, BLOCK)
        return remote(
            zs2.at[c % slots_z, g, :, there, :], zb2.at[c, z, g], z2_send.at[c, g], z2_recv.at[c], dev(dz=dz)
        )

    def wait_z2_sent(c, g):
        wait_bytes(zs2.at[c % slots_z, g, :, pl.ds(0, 3 * BLOCK), :], z2_send.at[c, g])

    def out_cols(c):
        return out_ref.at[:, pl.ds(pl.multiple_of(k * half_cols + c * WIDE, WIDE), WIDE)]

    def o_copy(c):
        return remote(fin.at[c, rows_of((1 - k) * TOKENS, TOKENS)], out_cols(c), o_sem.at[0], o_sem.at[1], dev(dk=1))

    def o_local(c):
        return pltpu.make_async_copy(fin.at[c, rows_of(k * TOKENS, TOKENS)], out_cols(c), o_sem.at[2])

    for j in (direct, 0, 1):
        local_w(j).start()
    for i in range(4):
        local_a(i).start()
    rest = [j for j in range(2, chunks) if j != direct]
    for j in rest:
        local_w(j).start()

    barrier = pltpu.get_barrier_semaphore()
    near = [dev(dx=i) for i in (1, 2, 3)] + [dev(dz=i) for i in (1, 2, 3)] + [dev(dy=a, dk=b) for a, b in peers]
    for to in near:
        pl.semaphore_signal(barrier, inc=1, device_id=to, device_id_type=MESH)

    ids = ids_ref[...]
    experts = lax.broadcasted_iota(jnp.int32, (EXPERTS, TOKENS), 0)
    ones = [ids[i:i + 1, :] == experts for i in range(2)]
    counts = (ones[0].astype(F32) + ones[1].astype(F32)).astype(BF)
    earlier = lax.broadcasted_iota(jnp.int32, (TOKENS, TOKENS), 0) < lax.broadcasted_iota(jnp.int32, (TOKENS, TOKENS), 1)
    before = jnp.dot(counts, earlier.astype(F32).astype(BF), preferred_element_type=F32)
    code_rows = []
    for i in range(2):
        position = jnp.sum(jnp.where(ones[i], before, 0.0), axis=0, keepdims=True).astype(jnp.int32)
        if i == 1:
            position = position + (ids[0:1, :] == ids[1:2, :]).astype(jnp.int32)
        expert = ids[i:i + 1, :]
        code_rows.append((expert % 2) * DEPTH + (expert // 2) * WINDOW + position)
    row = lax.broadcasted_iota(jnp.int32, (8, TOKENS), 0)
    keys[x, y * 2 + k] = jnp.where(row == 0, code_rows[0], code_rows[1])

    pl.semaphore_wait(barrier, len(near))
    core_w(direct).start()
    core_a(0).start()
    for j in (0, 1):
        core_w(j).start()
    for i in range(7):
        key_copy(i).start()
    for i in range(1, 4):
        core_a(i).start()
    for j in rest:
        core_w(j).start()

    def product(g, c):
        rows = rows_of(g * GROUP, GROUP)
        cols = rows_of(c * WIDE, WIDE)
        return nt_dot(a_buf[0, rows, :], w_buf[0, cols, :]) + nt_dot(a_buf[1, rows, :], w_buf[1, cols, :])

    def wait_a(i):
        local_a(i).wait()
        core_a(i).wait_recv()

    def wait_w(c):
        local_w(c).wait()
        core_w(c).wait_recv()

    def halves(acc):
        return [acc[:, :HALF], acc[:, HALF:]]

    def a0(c):
        wait_w(c)

        @pl.when(c >= slots_x)
        def _():
            wait_bytes(xs.at[c % slots_x, 0], xt_send.at[c - slots_x])

        for side, part in enumerate(halves(product((x + 2) % 4, c))):
            xs[c % slots_x, 0, side] = part.astype(BF)
            x_copy(c, 0, side).start()

    def a1(side, c):
        other = 1 - side

        if side == 0:
            @pl.when(c >= slots_x)
            def _():
                wait_bytes(xs.at[c % slots_x, 1], xp_send.at[c - slots_x])

        wait_through(xr, xt_recv, c, other)
        part = halves(product((x + 3) % 4 if side == 0 else (x + 1) % 4, c))
        xr[c, 0, other] = (part[other] + xr[c, 0, other].astype(F32)).astype(BF)
        xs[c % slots_x, 1, side] = part[side].astype(BF)
        x_copy(c, 2, other).start()
        x_copy(c, 1, side).start()

    def a2(c):
        wait_tree(xr, x_recv, c)
        for side, part in enumerate(halves(product(x, c))):
            total = part + (xr[c, 1, side].astype(F32) + xr[c, 2, side].astype(F32))
            xr[c, 1, side] = total.astype(BF)
        for i in range(3):
            z_copy(c, i).start()
        zb[c, z] = xr[c, 1, :, rows_of(z * BLOCK, BLOCK), :]

    def to_tokens(blocks, g, yy):
        rows = rows_of(yy * 64, WINDOW)
        values = jnp.concatenate(
            [jnp.concatenate([blocks(e)[side, rows, :] for e in range(4)], axis=0) for side in range(2)], axis=1
        )
        return jnp.dot(sel[g, yy], values, preferred_element_type=F32)

    def a_tokens(c, yy):
        return to_tokens(lambda e: zb.at[c, e], x, yy)

    def share_keys(_):
        wait_bytes(keys.at[x, pl.ds(0, 7)], key_sem.at[1])
        for i in range(3):
            group_copy(i).start()

    def build(part):
        @pl.when(part == 0)
        def _():
            wait_bytes(keys.at[pl.ds(0, 3)], key_sem.at[3])

        lanes = lax.broadcasted_iota(jnp.int32, (TOKENS, DEPTH), 1).astype(F32)

        def body(n):
            g, yy, kk = part, n // 2, n % 2
            turned = jnp.transpose(keys[g, yy * 2 + kk].astype(F32))
            shift = (yy * 4 + kk * SLOTS - (y // 2) * DEPTH).astype(F32)
            hit = (turned[:, 0:1] + shift == lanes) | (turned[:, 1:2] + shift == lanes)
            sel[g, yy, rows_of(kk * TOKENS, TOKENS), :] = hit.astype(F32).astype(BF)

        loop(8, body)

    def a3(c):
        wait_bytes(zb.at[c, pl.ds(0, 3)], z_recv.at[c])
        for side, part in enumerate(halves(a_tokens(c, (y + 2) % 4))):
            ys[c, 0, side] = part.astype(BF)
        y_copy(c, 0, 0).start()
        y_copy(c, 0, 1).start()

    def a4(c):
        for side in range(2):
            other = 1 - side
            part = halves(a_tokens(c, (y + 3) % 4 if side == 0 else (y + 1) % 4))
            ys[c, 1, side] = part[side].astype(BF)
            y_copy(c, 1, side).start()
            wait_through(yr, yt_recv, c, other)
            yr[c, 0, other] = (part[other] + yr[c, 0, other].astype(F32)).astype(BF)
            y_copy(c, 2, other).start()

    def deliver(c):
        o_copy(c).start()
        o_local(c).start()

    def a5(c):
        wait_tree(yr, y_recv, c)
        for side, part in enumerate(halves(a_tokens(c, y))):
            total = part + (yr[c, 1, side].astype(F32) + yr[c, 2, side].astype(F32))
            fin[c, :, side * HALF:(side + 1) * HALF] = total.astype(BF)
        deliver(c)

    def a6(c):
        wait_bytes(xr.at[c, 0], xc_send.at[c])
        wait_bytes(yr.at[c], y_send.at[c])
        wait_bytes(xr.at[c, 1, :, pl.ds(0, 3 * BLOCK), :], z_send.at[c])

    def e0(q):
        c, i = q // 4, q % 4
        g = nth_group(i)

        @pl.when(i == 0)
        def _():
            wait_w(direct + c)

        @pl.when(c == 0)
        def _():
            wait_a(i)

        @pl.when(c >= slots_z)
        def _():
            wait_z2_sent(c - slots_z, g)

        for side, part in enumerate(halves(product(g, direct + c))):
            zs2[c % slots_z, g, side] = part.astype(BF)
        for dz in (2, 1, 3):
            z2_copy(c, g, dz).start()
        zb2[c, z, g] = zs2[c % slots_z, g, :, rows_of(z * BLOCK, BLOCK), :]

    def e_tokens(c, g, yy):
        return to_tokens(lambda e: zb2.at[c, e, g], g, yy)

    def group_rows(g):
        return rows_of(g * 2 * TOKENS, 2 * TOKENS)

    def e1(c):
        wait_bytes(zb2.at[c, pl.ds(0, 3)], z2_recv.at[c])

        def body(g):
            for side, part in enumerate(halves(e_tokens(c, g, (y + 2) % 4))):
                ys2[c, 0, side, group_rows(g), :] = part.astype(BF)

        loop(4, body)
        y2_copy(c, 0, 0).start()
        y2_copy(c, 0, 1).start()

    def e2(c):
        for side in range(2):
            other = 1 - side
            wait_through(yr2, y2t_recv, c, other)

            def body(g):
                part = halves(e_tokens(c, g, (y + 3) % 4 if side == 0 else (y + 1) % 4))
                rows = group_rows(g)
                ys2[c, 1, side, rows, :] = part[side].astype(BF)
                yr2[c, 0, other, rows, :] = (part[other] + yr2[c, 0, other, rows, :].astype(F32)).astype(BF)

            loop(4, body)
            y2_copy(c, 2, other).start()
            y2_copy(c, 1, side).start()

    def e3(c):
        wait_tree(yr2, y2_recv, c)

        def body(g):
            rows = group_rows(g)
            for side, part in enumerate(halves(e_tokens(c, g, y))):
                total = part + (yr2[c, 1, side, rows, :].astype(F32) + yr2[c, 2, side, rows, :].astype(F32))
                ye2[c, g, side] = total.astype(BF)

        loop(4, body)
        for kind in range(2):
            for side in range(2):
                x2_copy(c, kind, side).start()

    def e4(c):
        for side in range(2):
            wait_through(xr2, x2t_recv, c, side)
            mine = ye2[c, (x + 1) % 4 if side == 0 else (x + 3) % 4, side]
            xr2[c, 0, side] = (mine.astype(F32) + xr2[c, 0, side].astype(F32)).astype(BF)
            x2_copy(c, 2, side).start()

    def e5(c):
        wait_tree(xr2, x2_recv, c)
        for side in range(2):
            total = ye2[c, x, side].astype(F32) + (xr2[c, 1, side].astype(F32) + xr2[c, 2, side].astype(F32))
            fin[direct + c, :, side * HALF:(side + 1) * HALF] = total.astype(BF)
        deliver(direct + c)

    def e6(c):
        wait_bytes(xr2.at[c], x2_send.at[c])
        wait_bytes(yr2.at[c], y2_send.at[c])

    def old_sends(_):
        wait_bytes(a_buf.at[1], core_send.at[0])
        wait_bytes(w_buf.at[1], core_send.at[1])
        wait_bytes(keys.at[x, pl.ds(0, 7)], key_sem.at[0])
        wait_bytes(keys.at[pl.ds(0, 3)], key_sem.at[2])

    def last_sends(_):
        for c in range(max(0, direct - slots_x), direct):
            wait_bytes(xs.at[c % slots_x, 0], xt_send.at[c])
            wait_bytes(xs.at[c % slots_x, 1], xp_send.at[c])
        for c in range(max(0, early - slots_z), early):
            for g in range(4):
                wait_z2_sent(c, g)

    plan = (
        (a0, (2, 3, 6, 10, 17)),
        (functools.partial(a1, 0), (11, 19, 20, 24, 25)),
        (functools.partial(a1, 1), (11, 19, 20, 24, 25)),
        (e0, (0, 3, 5, 7, 8, 9, 15, 16, 17, 21, 22, 27)),
        (share_keys, (1,)),
        (build, (4, 9, 12, 13)),
        (e1, (14, 23, 30)),
        (e2, (18, 26, 33)),
        (e3, (29, 39, 44)),
        (e4, (38, 42, 48)),
        (e5, (41, 49, 53)),
        (a2, (28, 31, 34, 35, 37)),
        (a3, (32, 34, 36, 43, 47)),
        (a4, (35, 40, 45, 50, 52)),
        (a5, (46, 51, 54, 55, 56)),
        (old_sends, (32,)),
        (last_sends, (41,)),
        (e6, (43, 51, 55)),
        (a6, (48, 53, 55, 56, 57)),
    )

    def step(n):
        for stage, steps in plan:
            now = [n == at for at in steps]

            @pl.when(functools.reduce(jnp.logical_or, now))
            def _():
                stage(sum(i * hit.astype(jnp.int32) for i, hit in enumerate(now)))

    loop(1 + max(max(steps) for _, steps in plan), step)
    mine = fin.at[:, pl.ds(0, TOKENS)]
    for i in range(3):
        wait_bytes(mine, o_sem.at[i])


def on_device(expert_ids, hidden_grad, up_weight):
    rows, hid = hidden_grad.shape
    width = up_weight.shape[0]
    chunks = width // 2 // WIDE
    early = 3
    direct = chunks - early
    dma = pltpu.SemaphoreType.DMA
    both = 2 * TOKENS

    def vmem(*shape):
        return pltpu.VMEM(shape, BF)

    out = pl.pallas_call(
        functools.partial(kernel, direct, early),
        out_shape=jax.ShapeDtypeStruct((TOKENS, width), BF),
        in_specs=[
            pl.BlockSpec(memory_space=pltpu.VMEM),
            pl.BlockSpec(memory_space=pl.ANY),
            pl.BlockSpec(memory_space=pl.ANY),
        ],
        out_specs=pl.BlockSpec(memory_space=pl.ANY),
        scratch_shapes=[
            vmem(2, rows, hid),
            vmem(2, width // 2, hid),
            vmem(3, 2, 2, GROUP, HALF),
            vmem(direct, 3, 2, GROUP, HALF),
            vmem(direct, 4, 2, BLOCK, HALF),
            vmem(direct, 2, 2, both, HALF),
            vmem(direct, 3, 2, both, HALF),
            vmem(2, 4, 2, GROUP, HALF),
            vmem(early, 4, 4, 2, BLOCK, HALF),
            vmem(early, 2, 2, 4 * both, HALF),
            vmem(early, 3, 2, 4 * both, HALF),
            vmem(early, 4, 2, both, HALF),
            vmem(early, 3, 2, both, HALF),
            vmem(4, 4, both, DEPTH),
            vmem(chunks, both, WIDE),
            pltpu.VMEM((4, SHARDS, 8, TOKENS), jnp.int32),
            dma((4 + chunks,)), dma((2,)), dma((4 + chunks,)), dma((4,)),
            dma((direct,)), dma((direct,)), dma((direct,)), dma((direct, 2)), dma((direct,)),
            dma((direct,)), dma((direct,)), dma((direct,)), dma((direct, 2)), dma((direct,)),
            dma((early, 4)), dma((early,)), dma((early,)), dma((early, 2)), dma((early,)),
            dma((early,)), dma((early, 2)), dma((early,)), dma((3,)),
        ],
        compiler_params=pltpu.CompilerParams(
            collective_id=0, has_side_effects=True, vmem_limit_bytes=63 * 2**20
        ),
        cost_estimate=pl.CostEstimate(
            flops=2 * rows * hid * width, bytes_accessed=2 * (rows + width) * hid + 2 * TOKENS * width, transcendentals=0
        ),
        name="up_cotangent",
    )(expert_ids[0].T, hidden_grad, up_weight)
    return out[None]


def solution(mesh):
    return jax.shard_map(
        on_device,
        mesh=mesh,
        in_specs=(P("dp", "expert", None), P(None, ("dp", "expert")), P(None, ("dp", "expert"))),
        out_specs=P("dp", "expert", None),
        check_vma=False,
    )
```

```python
import functools

import jax
import jax.numpy as jnp
from jax import lax
from jax.experimental import pallas as pl
from jax.experimental.pallas import tpu as pltpu
from jax.sharding import PartitionSpec as P

EXPERTS = 8
SLOTS = 34
SHARDS = 8
BLOCK = SLOTS * SHARDS
GROUP = 4 * BLOCK
WINDOW = 80
DEPTH = 4 * WINDOW
TOKENS = 128
WIDE = 256
HALF = 128
MESH = pl.DeviceIdType.MESH
BF = jnp.bfloat16
F32 = jnp.float32


def nt_dot(a, b):
    return lax.dot_general(a, b, (((1,), (1,)), ((), ())), preferred_element_type=F32)


def kernel(
    direct, early, ids_ref, hid_ref, w_ref, out_ref,
    a_buf, w_buf, xs, xr, zb, yr, zs2, zb2, ys2, yr2, ye2, xr2, sel, fin, keys,
    in_sem, core_send, core_recv, key_sem, xt_send, xp_send, xc_send, xt_recv, x_recv,
    z_send, z_recv, y_send, y_recv, z2_send, z2_recv, y2_send, y2t_recv, y2_recv, x2_send, x2t_recv, x2_recv, o_sem, a_sem,
):
    x = lax.axis_index("dp")
    col = lax.axis_index("expert")
    z, y, k = col // 8, (col // 2) % 4, col % 2
    chunks = direct + early
    half_cols = chunks * WIDE
    slots_x = xs.shape[0]
    slots_z = zs2.shape[0]

    def dev(dx=0, dz=0, dy=0, dk=0):
        return ((x + dx) % 4, ((z + dz) % 4) * 8 + ((y + dy) % 4) * 2 + (k + dk) % 2)

    def rows_of(start, size):
        return pl.ds(pl.multiple_of(start, 16), size)

    def remote(src, dst, send, recv, to):
        return pltpu.make_async_remote_copy(
            src_ref=src, dst_ref=dst, send_sem=send, recv_sem=recv, device_id=to, device_id_type=MESH
        )

    def loop(count, body):
        lax.fori_loop(0, count, lambda i, _: (body(i), 0)[1], 0)

    def nth_group(i):
        return (x + jnp.where(i < 2, i + 2, 3 - i)) % 4

    def local_a(i):
        rows = rows_of(nth_group(i) * GROUP, GROUP)
        return pltpu.make_async_copy(hid_ref.at[rows], a_buf.at[0, rows], in_sem.at[i])

    def local_w(j):
        return pltpu.make_async_copy(
            w_ref.at[rows_of(k * half_cols + j * WIDE, WIDE)], w_buf.at[0, rows_of(j * WIDE, WIDE)], in_sem.at[4 + j]
        )

    def core_a(i):
        rows = rows_of(nth_group(i) * GROUP, GROUP)
        return remote(hid_ref.at[rows], a_buf.at[1, rows], core_send.at[0], core_recv.at[i], dev(dk=1))

    def core_w(j):
        return remote(
            w_ref.at[rows_of((1 - k) * half_cols + j * WIDE, WIDE)],
            w_buf.at[1, rows_of(j * WIDE, WIDE)],
            core_send.at[1], core_recv.at[4 + j], dev(dk=1),
        )

    peers = [(dy, dk) for dy in range(4) for dk in range(2) if (dy, dk) != (0, 0)]

    def key_copy(i):
        dy, dk = peers[i]
        mine = y * 2 + k
        return remote(keys.at[x, mine], keys.at[x, mine], key_sem.at[0], key_sem.at[1], dev(dy=dy, dk=dk))

    def group_copy(i):
        return remote(keys.at[x], keys.at[x], key_sem.at[2], key_sem.at[3], dev(dx=i + 1))

    def wait_bytes(ref, sem):
        pltpu.make_async_copy(ref, ref, sem).wait()

    def tree_copy(source, recvs, s_sems, t_sem, r_sem, axis, by_side, c, kind, side):
        step = 1 if (side == 0) != (kind == 1) else -1
        src = recvs.at[c, 0, side] if kind == 2 else source(c, kind, side, step)
        return remote(
            src, recvs.at[c, kind, side], s_sems[kind].at[c],
            t_sem.at[c, side] if kind == 0 else r_sem.at[c, side] if by_side else r_sem.at[c], dev(**{axis: step}),
        )

    x_copy = functools.partial(
        tree_copy, lambda c, kind, side, step: xs.at[c % slots_x, kind, side], xr,
        (xt_send, xp_send, xc_send), xt_recv, x_recv, "dx", True,
    )
    def token_block(c, side, i, blocks=1):
        return xr.at[c, 2, side, rows_of(i * TOKENS, blocks * TOKENS), :]

    def y_copy(c, side, i):
        dy, dk = peers[i]
        return remote(
            token_block(c, side, (y + dy) % 4 * 2 + (k + dk) % 2), yr.at[c, side, k * 4 + y],
            y_send.at[c, side], y_recv.at[c, side], dev(dy=dy, dk=dk),
        )

    y2_copy = functools.partial(
        tree_copy, lambda c, kind, side, step: ys2.at[c, kind, side], yr2, (y2_send,) * 3, y2t_recv, y2_recv, "dy", False
    )
    x2_copy = functools.partial(
        tree_copy, lambda c, kind, side, step: ye2.at[c, (x + (step if kind else 2)) % 4, side], xr2,
        (x2_send,) * 3, x2t_recv, x2_recv, "dx", False,
    )

    def wait_through(recvs, t_sem, c, side):
        wait_bytes(recvs.at[c, 0, side], t_sem.at[c, side])

    def wait_tree(recvs, r_sem, c):
        wait_bytes(recvs.at[c, pl.ds(1, 2)], r_sem.at[c])

    def z_copy(c, side, dz):
        there = rows_of(((z + dz) % 4) * BLOCK, BLOCK)
        return remote(
            xr.at[c, 1, side, there, :], zb.at[c, z, side], z_send.at[c, side], z_recv.at[c, side], dev(dz=dz)
        )

    def z2_copy(c, g, dz):
        there = rows_of(((z + dz) % 4) * BLOCK, BLOCK)
        return remote(
            zs2.at[c % slots_z, g, :, there, :], zb2.at[c, z, g], z2_send.at[c, g], z2_recv.at[c, g], dev(dz=dz)
        )

    def wait_z2_sent(c, g):
        wait_bytes(zs2.at[c % slots_z, g, :, pl.ds(0, 3 * BLOCK), :], z2_send.at[c, g])

    def out_cols(c):
        return out_ref.at[:, pl.ds(pl.multiple_of(k * half_cols + (direct + c) * WIDE, WIDE), WIDE)]

    def o_copy(c):
        return remote(fin.at[c, rows_of((1 - k) * TOKENS, TOKENS)], out_cols(c), o_sem.at[0], o_sem.at[1], dev(dk=1))

    def o_local(c):
        return pltpu.make_async_copy(fin.at[c, rows_of(k * TOKENS, TOKENS)], out_cols(c), o_sem.at[2])

    for j in (direct, 0, 1):
        local_w(j).start()
    for i in range(4):
        local_a(i).start()
    rest = [j for j in range(2, chunks) if j != direct]
    for j in rest:
        local_w(j).start()

    barrier = pltpu.get_barrier_semaphore()
    near = [dev(dx=i) for i in (1, 2, 3)] + [dev(dz=i) for i in (1, 2, 3)] + [dev(dy=a, dk=b) for a, b in peers]
    for to in near:
        pl.semaphore_signal(barrier, inc=1, device_id=to, device_id_type=MESH)

    ids = ids_ref[...]
    experts = lax.broadcasted_iota(jnp.int32, (EXPERTS, TOKENS), 0)
    ones = [ids[i:i + 1, :] == experts for i in range(2)]
    counts = (ones[0].astype(F32) + ones[1].astype(F32)).astype(BF)
    earlier = lax.broadcasted_iota(jnp.int32, (TOKENS, TOKENS), 0) < lax.broadcasted_iota(jnp.int32, (TOKENS, TOKENS), 1)
    before = jnp.dot(counts, earlier.astype(F32).astype(BF), preferred_element_type=F32)
    code_rows = []
    for i in range(2):
        position = jnp.sum(jnp.where(ones[i], before, 0.0), axis=0, keepdims=True).astype(jnp.int32)
        if i == 1:
            position = position + (ids[0:1, :] == ids[1:2, :]).astype(jnp.int32)
        expert = ids[i:i + 1, :]
        code_rows.append((expert % 2) * DEPTH + (expert // 2) * WINDOW + position)
    row = lax.broadcasted_iota(jnp.int32, (8, TOKENS), 0)
    keys[x, y * 2 + k] = jnp.where(row == 0, code_rows[0], code_rows[1])

    pl.semaphore_wait(barrier, len(near))
    core_w(direct).start()
    core_a(0).start()
    for j in (0, 1):
        core_w(j).start()
    for i in range(7):
        key_copy(i).start()
    for i in range(1, 4):
        core_a(i).start()
    for j in rest:
        core_w(j).start()

    def product(g, c, r=0, parts=1):
        rows = rows_of(g * GROUP + r * (GROUP // parts), GROUP // parts)
        cols = rows_of(c * WIDE, WIDE)
        return nt_dot(a_buf[0, rows, :], w_buf[0, cols, :]) + nt_dot(a_buf[1, rows, :], w_buf[1, cols, :])

    def wait_a(i):
        local_a(i).wait()
        core_a(i).wait_recv()

    def wait_w(c):
        local_w(c).wait()
        core_w(c).wait_recv()

    def halves(acc):
        return [acc[:, :HALF], acc[:, HALF:]]

    def a0(c):
        wait_w(c)

        @pl.when(c >= slots_x)
        def _():
            wait_bytes(xs.at[c % slots_x, 0], xt_send.at[c - slots_x])

        for side, part in enumerate(halves(product((x + 2) % 4, c))):
            xs[c % slots_x, 0, side] = part.astype(BF)
            x_copy(c, 0, side).start()

    def a1(side, c):
        other = 1 - side

        if side == 0:
            @pl.when(c >= slots_x)
            def _():
                wait_bytes(xs.at[c % slots_x, 1], xp_send.at[c - slots_x])

        wait_through(xr, xt_recv, c, other)
        def body(r):
            part = halves(product((x + 3) % 4 if side == 0 else (x + 1) % 4, c, r, 2))
            rows = rows_of(r * (GROUP // 2), GROUP // 2)
            xr[c, 0, other, rows] = (part[other] + xr[c, 0, other, rows].astype(F32)).astype(BF)
            xs[c % slots_x, 1, side, rows] = part[side].astype(BF)

        loop(2, body)
        for kind, at in ((1, 0), (2, 1)) if side == 0 else ((2, 0), (1, 1)):
            x_copy(c, kind, at).start()

    def a2(h):
        c, side = h // 2, h % 2
        wait_bytes(xr.at[c, pl.ds(1, 2), side], x_recv.at[c, side])
        rows = rows_of(x * GROUP, GROUP)
        cols = rows_of(c * WIDE + side * HALF, HALF)
        own = nt_dot(a_buf[0, rows, :], w_buf[0, cols, :]) + nt_dot(a_buf[1, rows, :], w_buf[1, cols, :])
        total = own + (xr[c, 1, side].astype(F32) + xr[c, 2, side].astype(F32))
        xr[c, 1, side] = total.astype(BF)
        for dz in (2, 1, 3):
            z_copy(c, side, dz).start()
        zb[c, z, side] = xr[c, 1, side, rows_of(z * BLOCK, BLOCK), :]

    def to_tokens(blocks, g, yy):
        rows = rows_of(yy * 64, WINDOW)
        values = jnp.concatenate(
            [jnp.concatenate([blocks(e)[side, rows, :] for e in range(4)], axis=0) for side in range(2)], axis=1
        )
        return jnp.dot(sel[g, yy], values, preferred_element_type=F32)

    def share_keys(_):
        wait_bytes(keys.at[x, pl.ds(0, 7)], key_sem.at[1])
        for i in range(3):
            group_copy(i).start()

    def build(part):
        @pl.when(part == 0)
        def _():
            wait_bytes(keys.at[pl.ds(0, 3)], key_sem.at[3])

        lanes = lax.broadcasted_iota(jnp.int32, (TOKENS, DEPTH), 1).astype(F32)

        def body(n):
            g, yy, kk = part, n // 2, n % 2
            turned = jnp.transpose(keys[g, yy * 2 + kk].astype(F32))
            shift = (yy * 4 + kk * SLOTS - (y // 2) * DEPTH).astype(F32)
            hit = (turned[:, 0:1] + shift == lanes) | (turned[:, 1:2] + shift == lanes)
            sel[g, yy, rows_of(kk * TOKENS, TOKENS), :] = hit.astype(F32).astype(BF)

        loop(8, body)

    def a3(h):
        c, side = h // 2, h % 2
        wait_bytes(zb.at[c, pl.ds(0, 3), side], z_recv.at[c, side])

        def body(yy):
            rows = rows_of(yy * 64, WINDOW)
            values = jnp.concatenate([zb[c, e, side, rows, :] for e in range(4)], axis=0)
            acc = jnp.dot(sel[x, yy], values, preferred_element_type=F32).astype(BF)
            token_block(c, side, yy * 2, 2)[...] = acc

        loop(4, body)
        for i in (3, 4, 1, 2, 5, 6, 0):
            y_copy(c, side, i).start()
        yr[c, side, k * 4 + y] = token_block(c, side, y * 2 + k)[...]

    def a_local(c, side, core):
        cols = pl.ds(pl.multiple_of(core * half_cols + c * WIDE + side * HALF, HALF), HALF)
        return pltpu.make_async_copy(yr.at[c, side, core * 4], out_ref.at[:, cols], a_sem.at[0])

    def a4(h):
        c, side = h // 2, h % 2
        wait_bytes(yr.at[c, side, pl.ds(0, 7)], y_recv.at[c, side])
        for core in range(2):
            parts = [yr[c, side, core * 4 + i].astype(F32) for i in range(4)]
            yr[c, side, core * 4] = ((parts[0] + parts[1]) + (parts[2] + parts[3])).astype(BF)
            a_local(c, side, core).start()

    def a5(c):
        wait_bytes(xr.at[c, 0], xc_send.at[c])
        for side in range(2):
            wait_bytes(token_block(c, side, 0, 7), y_send.at[c, side])
            wait_bytes(xr.at[c, 1, side, pl.ds(0, 3 * BLOCK), :], z_send.at[c, side])

    def e0(q):
        c, i = q // 4, q % 4
        g = nth_group(i)

        @pl.when(i == 0)
        def _():
            wait_w(direct + c)

        @pl.when(c == 0)
        def _():
            wait_a(i)

        @pl.when(c >= slots_z)
        def _():
            wait_z2_sent(c - slots_z, g)

        for side, part in enumerate(halves(product(g, direct + c))):
            zs2[c % slots_z, g, side] = part.astype(BF)
        for dz in (2, 1, 3):
            z2_copy(c, g, dz).start()
        zb2[c, z, g] = zs2[c % slots_z, g, :, rows_of(z * BLOCK, BLOCK), :]

    def e_tokens(c, g, yy):
        return to_tokens(lambda e: zb2.at[c, e, g], g, yy)

    def e1(q):
        c, g = q // 4, nth_group(q % 4)
        at = c * 4 + g
        wait_bytes(zb2.at[c, pl.ds(0, 3), g], z2_recv.at[c, g])
        for side, part in enumerate(halves(e_tokens(c, g, (y + 2) % 4))):
            ys2[at, 0, side] = part.astype(BF)
        for side in range(2):
            y2_copy(at, 0, side).start()

    def e2(q):
        c, g = q // 4, nth_group(q % 4)
        at = c * 4 + g
        for side in range(2):
            other = 1 - side
            part = halves(e_tokens(c, g, (y + 3) % 4 if side == 0 else (y + 1) % 4))
            ys2[at, 1, side] = part[side].astype(BF)
            wait_through(yr2, y2t_recv, at, other)
            yr2[at, 0, other] = (part[other] + yr2[at, 0, other].astype(F32)).astype(BF)
            y2_copy(at, 2, other).start()
            y2_copy(at, 1, side).start()

    def e3(q):
        c, i = q // 4, q % 4
        g = nth_group(i)
        at = c * 4 + g
        wait_tree(yr2, y2_recv, at)
        for side, part in enumerate(halves(e_tokens(c, g, y))):
            total = part + (yr2[at, 1, side].astype(F32) + yr2[at, 2, side].astype(F32))
            ye2[c, g, side] = total.astype(BF)
        for first, kind, side in ((0, 0, 0), (0, 0, 1), (1, 1, 0), (2, 1, 1)):
            @pl.when(i == first)
            def _():
                x2_copy(c, kind, side).start()

    def e4(c):
        for side in range(2):
            wait_through(xr2, x2t_recv, c, side)
            mine = ye2[c, (x + 1) % 4 if side == 0 else (x + 3) % 4, side]
            xr2[c, 0, side] = (mine.astype(F32) + xr2[c, 0, side].astype(F32)).astype(BF)
            x2_copy(c, 2, side).start()

    def e5(c):
        wait_tree(xr2, x2_recv, c)
        for side in range(2):
            total = ye2[c, x, side].astype(F32) + (xr2[c, 1, side].astype(F32) + xr2[c, 2, side].astype(F32))
            fin[c, :, side * HALF:(side + 1) * HALF] = total.astype(BF)
        o_copy(c).start()
        o_local(c).start()

    def e6(c):
        wait_bytes(xr2.at[c], x2_send.at[c])
        for g in range(4):
            wait_bytes(yr2.at[c * 4 + g], y2_send.at[c * 4 + g])

    def old_sends(_):
        wait_bytes(a_buf.at[1], core_send.at[0])
        wait_bytes(w_buf.at[1], core_send.at[1])
        wait_bytes(keys.at[x, pl.ds(0, 7)], key_sem.at[0])
        wait_bytes(keys.at[pl.ds(0, 3)], key_sem.at[2])

    def last_sends(_):
        for c in range(max(0, direct - slots_x), direct):
            wait_bytes(xs.at[c % slots_x, 0], xt_send.at[c])
            wait_bytes(xs.at[c % slots_x, 1], xp_send.at[c])
        for c in range(max(0, early - slots_z), early):
            for g in range(4):
                wait_z2_sent(c, g)

    plan = (
        (a0, (1, 3, 5, 7, 12)),
        (functools.partial(a1, 0), (4, 6, 17, 27, 28)),
        (functools.partial(a1, 1), (4, 6, 17, 27, 28)),
        (e0, (0, 1, 2, 5, 7, 8, 11, 13, 16, 19, 20, 23)),
        (share_keys, (0,)),
        (build, (3, 5, 7, 8)),
        (e1, (8, 9, 10, 11, 13, 18, 22, 24, 27, 28, 31, 36)),
        (e2, (11, 13, 14, 15, 19, 23, 25, 27, 28, 30, 34, 41)),
        (e3, (26, 28, 29, 35, 37, 38, 39, 40, 46, 51, 52, 54)),
        (e4, (33, 48, 52)),
        (e5, (46, 50, 55)),
        (a2, (19, 21, 23, 24, 29, 32, 36, 42, 44, 47)),
        (a3, (31, 34, 38, 42, 43, 44, 45, 47, 49, 50)),
        (a4, (36, 44, 47, 50, 51, 53, 54, 55, 56, 57)),
        (old_sends, (37,)),
        (last_sends, (51,)),
        (e6, (48, 52, 57)),
        (a5, (46, 52, 55, 57, 58)),
    )

    def step(n):
        for stage, steps in plan:
            now = [n == at for at in steps]

            @pl.when(functools.reduce(jnp.logical_or, now))
            def _():
                stage(sum(i * hit.astype(jnp.int32) for i, hit in enumerate(now)))

    loop(1 + max(max(steps) for _, steps in plan), step)
    mine = fin.at[:, pl.ds(0, TOKENS)]
    for i in range(3):
        wait_bytes(mine, o_sem.at[i])
    wait_bytes(yr.at[:, :, pl.ds(0, 2)], a_sem.at[0])


def on_device(expert_ids, hidden_grad, up_weight):
    rows, hid = hidden_grad.shape
    width = up_weight.shape[0]
    chunks = width // 2 // WIDE
    early = 3
    direct = chunks - early
    dma = pltpu.SemaphoreType.DMA
    both = 2 * TOKENS

    def vmem(*shape):
        return pltpu.VMEM(shape, BF)

    out = pl.pallas_call(
        functools.partial(kernel, direct, early),
        out_shape=jax.ShapeDtypeStruct((TOKENS, width), BF),
        in_specs=[
            pl.BlockSpec(memory_space=pltpu.VMEM),
            pl.BlockSpec(memory_space=pl.ANY),
            pl.BlockSpec(memory_space=pl.ANY),
        ],
        out_specs=pl.BlockSpec(memory_space=pl.ANY),
        scratch_shapes=[
            vmem(2, rows, hid),
            vmem(2, width // 2, hid),
            vmem(3, 2, 2, GROUP, HALF),
            vmem(direct, 3, 2, GROUP, HALF),
            vmem(direct, 4, 2, BLOCK, HALF),
            vmem(direct, 2, SHARDS, TOKENS, HALF),
            vmem(2, 4, 2, GROUP, HALF),
            vmem(early, 4, 4, 2, BLOCK, HALF),
            vmem(early * 4, 2, 2, both, HALF),
            vmem(early * 4, 3, 2, both, HALF),
            vmem(early, 4, 2, both, HALF),
            vmem(early, 3, 2, both, HALF),
            vmem(4, 4, both, DEPTH),
            vmem(early, both, WIDE),
            pltpu.VMEM((4, SHARDS, 8, TOKENS), jnp.int32),
            dma((4 + chunks,)), dma((2,)), dma((4 + chunks,)), dma((4,)),
            dma((direct,)), dma((direct,)), dma((direct,)), dma((direct, 2)), dma((direct, 2)),
            dma((direct, 2)), dma((direct, 2)), dma((direct, 2)), dma((direct, 2)),
            dma((early, 4)), dma((early, 4)), dma((early * 4,)), dma((early * 4, 2)), dma((early * 4,)),
            dma((early,)), dma((early, 2)), dma((early,)), dma((3,)), dma((1,)),
        ],
        compiler_params=pltpu.CompilerParams(
            collective_id=0, has_side_effects=True, vmem_limit_bytes=63 * 2**20
        ),
        cost_estimate=pl.CostEstimate(
            flops=2 * rows * hid * width, bytes_accessed=2 * (rows + width) * hid + 2 * TOKENS * width, transcendentals=0
        ),
        name="up_cotangent",
    )(expert_ids[0].T, hidden_grad, up_weight)
    return out[None]


def solution(mesh):
    return jax.shard_map(
        on_device,
        mesh=mesh,
        in_specs=(P("dp", "expert", None), P(None, ("dp", "expert")), P(None, ("dp", "expert"))),
        out_specs=P("dp", "expert", None),
        check_vma=False,
    )
```

```python
import functools

import jax
import jax.numpy as jnp
from jax import lax
from jax.experimental import pallas as pl
from jax.experimental.pallas import tpu as pltpu
from jax.sharding import PartitionSpec as P

EXPERTS = 8
SLOTS = 34
SHARDS = 8
BLOCK = SLOTS * SHARDS
GROUP = 4 * BLOCK
WINDOW = 80
DEPTH = 4 * WINDOW
TOKENS = 128
WIDE = 256
HALF = 128
MESH = pl.DeviceIdType.MESH
BF = jnp.bfloat16
F32 = jnp.float32


def nt_dot(a, b):
    return lax.dot_general(a, b, (((1,), (1,)), ((), ())), preferred_element_type=F32)


def kernel(
    direct, early, ids_ref, hid_ref, w_ref, out_ref,
    a_buf, w_buf, xs, xr, zb, yr, zs2, zb2, ys2, yr2, ye2, xr2, sel, fin, keys,
    in_sem, core_send, core_recv, key_sem, xt_send, xp_send, xc_send, xt_recv, x_recv,
    z_send, z_recv, y_send, y_recv, z2_send, z2_recv, y2_send, y2t_recv, y2_recv, x2_send, x2t_recv, x2_recv, o_sem, a_sem,
):
    x = lax.axis_index("dp")
    col = lax.axis_index("expert")
    z, y, k = col // 8, (col // 2) % 4, col % 2
    chunks = direct + early
    half_cols = chunks * WIDE
    slots_x = xs.shape[0]
    slots_z = zs2.shape[0]

    def dev(dx=0, dz=0, dy=0, dk=0):
        return ((x + dx) % 4, ((z + dz) % 4) * 8 + ((y + dy) % 4) * 2 + (k + dk) % 2)

    def rows_of(start, size):
        return pl.ds(pl.multiple_of(start, 16), size)

    def remote(src, dst, send, recv, to):
        return pltpu.make_async_remote_copy(
            src_ref=src, dst_ref=dst, send_sem=send, recv_sem=recv, device_id=to, device_id_type=MESH
        )

    def loop(count, body):
        lax.fori_loop(0, count, lambda i, _: (body(i), 0)[1], 0)

    def nth_group(i):
        return (x + jnp.where(i < 2, i + 2, 3 - i)) % 4

    def local_a(i):
        rows = rows_of(nth_group(i) * GROUP, GROUP)
        return pltpu.make_async_copy(hid_ref.at[rows], a_buf.at[0, rows], in_sem.at[i])

    def local_w(j):
        return pltpu.make_async_copy(
            w_ref.at[rows_of(k * half_cols + j * WIDE, WIDE)], w_buf.at[0, rows_of(j * WIDE, WIDE)], in_sem.at[4 + j]
        )

    def core_a(i):
        rows = rows_of(nth_group(i) * GROUP, GROUP)
        return remote(hid_ref.at[rows], a_buf.at[1, rows], core_send.at[0], core_recv.at[i], dev(dk=1))

    def core_w(j):
        return remote(
            w_ref.at[rows_of((1 - k) * half_cols + j * WIDE, WIDE)],
            w_buf.at[1, rows_of(j * WIDE, WIDE)],
            core_send.at[1], core_recv.at[4 + j], dev(dk=1),
        )

    peers = [(dy, dk) for dy in range(4) for dk in range(2) if (dy, dk) != (0, 0)]

    def key_copy(i):
        dy, dk = peers[i]
        mine = y * 2 + k
        return remote(keys.at[x, mine], keys.at[x, mine], key_sem.at[0], key_sem.at[1], dev(dy=dy, dk=dk))

    def group_copy(i):
        return remote(keys.at[x], keys.at[x], key_sem.at[2], key_sem.at[3], dev(dx=i + 1))

    def wait_bytes(ref, sem):
        pltpu.make_async_copy(ref, ref, sem).wait()

    def tree_copy(source, recvs, s_sems, t_sem, r_sem, axis, by_side, c, kind, side):
        step = 1 if (side == 0) != (kind == 1) else -1
        src = recvs.at[c, 0, side] if kind == 2 else source(c, kind, side, step)
        return remote(
            src, recvs.at[c, kind, side], s_sems[kind].at[c],
            t_sem.at[c, side] if kind == 0 else r_sem.at[c, side] if by_side else r_sem.at[c], dev(**{axis: step}),
        )

    x_copy = functools.partial(
        tree_copy, lambda c, kind, side, step: xs.at[c % slots_x, kind, side], xr,
        (xt_send, xp_send, xc_send), xt_recv, x_recv, "dx", True,
    )
    def token_block(c, side, i, blocks=1):
        return xr.at[c, 2, side, rows_of(i * TOKENS, blocks * TOKENS), :]

    def y_copy(c, side, i):
        dy, dk = peers[i]
        return remote(
            token_block(c, side, (y + dy) % 4 * 2 + (k + dk) % 2), yr.at[c, side, k * 4 + y],
            y_send.at[c, side], y_recv.at[c, side], dev(dy=dy, dk=dk),
        )

    y2_copy = functools.partial(
        tree_copy, lambda c, kind, side, step: ys2.at[c, kind, side], yr2, (y2_send,) * 3, y2t_recv, y2_recv, "dy", False
    )
    x2_copy = functools.partial(
        tree_copy, lambda c, kind, side, step: ye2.at[c, (x + (step if kind else 2)) % 4, side], xr2,
        (x2_send,) * 3, x2t_recv, x2_recv, "dx", False,
    )

    def wait_through(recvs, t_sem, c, side):
        wait_bytes(recvs.at[c, 0, side], t_sem.at[c, side])

    def wait_tree(recvs, r_sem, c):
        wait_bytes(recvs.at[c, pl.ds(1, 2)], r_sem.at[c])

    def z_copy(c, side, dz):
        there = rows_of(((z + dz) % 4) * BLOCK, BLOCK)
        return remote(
            xr.at[c, 1, side, there, :], zb.at[c, z, side], z_send.at[c, side], z_recv.at[c, side], dev(dz=dz)
        )

    def z2_copy(c, g, dz):
        there = rows_of(((z + dz) % 4) * BLOCK, BLOCK)
        return remote(
            zs2.at[c % slots_z, g, :, there, :], zb2.at[c, z, g], z2_send.at[c, g], z2_recv.at[c, g], dev(dz=dz)
        )

    def wait_z2_sent(c, g):
        wait_bytes(zs2.at[c % slots_z, g, :, pl.ds(0, 3 * BLOCK), :], z2_send.at[c, g])

    def out_cols(c):
        return out_ref.at[:, pl.ds(pl.multiple_of(k * half_cols + (direct + c) * WIDE, WIDE), WIDE)]

    def o_copy(c):
        return remote(fin.at[c, rows_of((1 - k) * TOKENS, TOKENS)], out_cols(c), o_sem.at[0], o_sem.at[1], dev(dk=1))

    def o_local(c):
        return pltpu.make_async_copy(fin.at[c, rows_of(k * TOKENS, TOKENS)], out_cols(c), o_sem.at[2])

    for j in (direct, 0, 1):
        local_w(j).start()
    for i in range(4):
        local_a(i).start()
    rest = [j for j in range(2, chunks) if j != direct]
    for j in rest:
        local_w(j).start()

    barrier = pltpu.get_barrier_semaphore()
    near = [dev(dx=i) for i in (1, 2, 3)] + [dev(dz=i) for i in (1, 2, 3)] + [dev(dy=a, dk=b) for a, b in peers]
    for to in near:
        pl.semaphore_signal(barrier, inc=1, device_id=to, device_id_type=MESH)

    ids = ids_ref[...]
    experts = lax.broadcasted_iota(jnp.int32, (EXPERTS, TOKENS), 0)
    ones = [ids[i:i + 1, :] == experts for i in range(2)]
    counts = (ones[0].astype(F32) + ones[1].astype(F32)).astype(BF)
    earlier = lax.broadcasted_iota(jnp.int32, (TOKENS, TOKENS), 0) < lax.broadcasted_iota(jnp.int32, (TOKENS, TOKENS), 1)
    before = jnp.dot(counts, earlier.astype(F32).astype(BF), preferred_element_type=F32)
    code_rows = []
    for i in range(2):
        position = jnp.sum(jnp.where(ones[i], before, 0.0), axis=0, keepdims=True).astype(jnp.int32)
        if i == 1:
            position = position + (ids[0:1, :] == ids[1:2, :]).astype(jnp.int32)
        expert = ids[i:i + 1, :]
        code_rows.append((expert % 2) * DEPTH + (expert // 2) * WINDOW + position)
    row = lax.broadcasted_iota(jnp.int32, (8, TOKENS), 0)
    keys[x, y * 2 + k] = jnp.where(row == 0, code_rows[0], code_rows[1])

    pl.semaphore_wait(barrier, len(near))
    core_w(direct).start()
    core_a(0).start()
    for j in (0, 1):
        core_w(j).start()
    for i in range(7):
        key_copy(i).start()
    for i in range(1, 4):
        core_a(i).start()
    for j in rest:
        core_w(j).start()

    def product(g, c, r=0, parts=1):
        rows = rows_of(g * GROUP + r * (GROUP // parts), GROUP // parts)
        cols = rows_of(c * WIDE, WIDE)
        return nt_dot(a_buf[0, rows, :], w_buf[0, cols, :]) + nt_dot(a_buf[1, rows, :], w_buf[1, cols, :])

    def wait_a(i):
        local_a(i).wait()
        core_a(i).wait_recv()

    def wait_w(c):
        local_w(c).wait()
        core_w(c).wait_recv()

    def halves(acc):
        return [acc[:, :HALF], acc[:, HALF:]]

    def a0(c):
        wait_w(c)

        @pl.when(c >= slots_x)
        def _():
            wait_bytes(xs.at[c % slots_x, 0], xt_send.at[c - slots_x])

        for side, part in enumerate(halves(product((x + 2) % 4, c))):
            xs[c % slots_x, 0, side] = part.astype(BF)
            x_copy(c, 0, side).start()

    def a1(side, c):
        other = 1 - side

        if side == 0:
            @pl.when(c >= slots_x)
            def _():
                wait_bytes(xs.at[c % slots_x, 1], xp_send.at[c - slots_x])

        wait_through(xr, xt_recv, c, other)
        def body(r):
            part = halves(product((x + 3) % 4 if side == 0 else (x + 1) % 4, c, r, 2))
            rows = rows_of(r * (GROUP // 2), GROUP // 2)
            xr[c, 0, other, rows] = (part[other] + xr[c, 0, other, rows].astype(F32)).astype(BF)
            xs[c % slots_x, 1, side, rows] = part[side].astype(BF)

        loop(2, body)
        for kind, at in ((1, 0), (2, 1)) if side == 0 else ((2, 0), (1, 1)):
            x_copy(c, kind, at).start()

    def a2(h):
        c, side = h // 2, h % 2
        wait_bytes(xr.at[c, pl.ds(1, 2), side], x_recv.at[c, side])
        rows = rows_of(x * GROUP, GROUP)
        cols = rows_of(c * WIDE + side * HALF, HALF)
        own = nt_dot(a_buf[0, rows, :], w_buf[0, cols, :]) + nt_dot(a_buf[1, rows, :], w_buf[1, cols, :])
        total = own + (xr[c, 1, side].astype(F32) + xr[c, 2, side].astype(F32))
        xr[c, 1, side] = total.astype(BF)
        for dz in (2, 1, 3):
            z_copy(c, side, dz).start()
        zb[c, z, side] = xr[c, 1, side, rows_of(z * BLOCK, BLOCK), :]

    def to_tokens(blocks, g, yy):
        rows = rows_of(yy * 64, WINDOW)
        values = jnp.concatenate(
            [jnp.concatenate([blocks(e)[side, rows, :] for e in range(4)], axis=0) for side in range(2)], axis=1
        )
        return jnp.dot(sel[g, yy], values, preferred_element_type=F32)

    def share_keys(_):
        wait_bytes(keys.at[x, pl.ds(0, 7)], key_sem.at[1])
        for i in range(3):
            group_copy(i).start()

    def build(part):
        @pl.when(part == 0)
        def _():
            wait_bytes(keys.at[pl.ds(0, 3)], key_sem.at[3])

        lanes = lax.broadcasted_iota(jnp.int32, (TOKENS, DEPTH), 1).astype(F32)

        def body(n):
            g, yy, kk = part, n // 2, n % 2
            turned = jnp.transpose(keys[g, yy * 2 + kk].astype(F32))
            shift = (yy * 4 + kk * SLOTS - (y // 2) * DEPTH).astype(F32)
            hit = (turned[:, 0:1] + shift == lanes) | (turned[:, 1:2] + shift == lanes)
            sel[g, yy, rows_of(kk * TOKENS, TOKENS), :] = hit.astype(F32).astype(BF)

        loop(8, body)

    def a3(h):
        c, side = h // 2, h % 2
        wait_bytes(zb.at[c, pl.ds(0, 3), side], z_recv.at[c, side])

        def body(yy):
            rows = rows_of(yy * 64, WINDOW)
            values = jnp.concatenate([zb[c, e, side, rows, :] for e in range(4)], axis=0)
            acc = jnp.dot(sel[x, yy], values, preferred_element_type=F32).astype(BF)
            token_block(c, side, yy * 2, 2)[...] = acc

        loop(4, body)
        for i in (3, 4, 1, 2, 5, 6, 0):
            y_copy(c, side, i).start()
        yr[c, side, k * 4 + y] = token_block(c, side, y * 2 + k)[...]

    def a_local(c, side, core):
        cols = pl.ds(pl.multiple_of(core * half_cols + c * WIDE + side * HALF, HALF), HALF)
        return pltpu.make_async_copy(yr.at[c, side, core * 4], out_ref.at[:, cols], a_sem.at[0])

    def a4(h):
        c, side = h // 2, h % 2
        wait_bytes(yr.at[c, side, pl.ds(0, 7)], y_recv.at[c, side])
        for core in range(2):
            parts = [yr[c, side, core * 4 + i].astype(F32) for i in range(4)]
            yr[c, side, core * 4] = ((parts[0] + parts[1]) + (parts[2] + parts[3])).astype(BF)
            a_local(c, side, core).start()

    def a5(c):
        wait_bytes(xr.at[c, 0], xc_send.at[c])
        for side in range(2):
            wait_bytes(token_block(c, side, 0, 7), y_send.at[c, side])
            wait_bytes(xr.at[c, 1, side, pl.ds(0, 3 * BLOCK), :], z_send.at[c, side])

    def e0(q):
        c, i = q // 4, q % 4
        g = nth_group(i)

        @pl.when(i == 0)
        def _():
            wait_w(direct + c)

        @pl.when(c == 0)
        def _():
            wait_a(i)

        @pl.when(c >= slots_z)
        def _():
            wait_z2_sent(c - slots_z, g)

        for side, part in enumerate(halves(product(g, direct + c))):
            zs2[c % slots_z, g, side] = part.astype(BF)
        for dz in (2, 1, 3):
            z2_copy(c, g, dz).start()
        zb2[c, z, g] = zs2[c % slots_z, g, :, rows_of(z * BLOCK, BLOCK), :]

    def e_tokens(c, g, yy):
        return to_tokens(lambda e: zb2.at[c, e, g], g, yy)

    def e1(q):
        c, g = q // 4, nth_group(q % 4)
        at = c * 4 + g
        wait_bytes(zb2.at[c, pl.ds(0, 3), g], z2_recv.at[c, g])
        for side, part in enumerate(halves(e_tokens(c, g, (y + 2) % 4))):
            ys2[at, 0, side] = part.astype(BF)
        for side in range(2):
            y2_copy(at, 0, side).start()

    def e2(q):
        c, g = q // 4, nth_group(q % 4)
        at = c * 4 + g
        for side in range(2):
            other = 1 - side
            part = halves(e_tokens(c, g, (y + 3) % 4 if side == 0 else (y + 1) % 4))
            ys2[at, 1, side] = part[side].astype(BF)
            wait_through(yr2, y2t_recv, at, other)
            yr2[at, 0, other] = (part[other] + yr2[at, 0, other].astype(F32)).astype(BF)
            y2_copy(at, 2, other).start()
            y2_copy(at, 1, side).start()

    def e3(q):
        c, i = q // 4, q % 4
        g = nth_group(i)
        at = c * 4 + g
        wait_tree(yr2, y2_recv, at)
        for side, part in enumerate(halves(e_tokens(c, g, y))):
            total = part + (yr2[at, 1, side].astype(F32) + yr2[at, 2, side].astype(F32))
            ye2[c, g, side] = total.astype(BF)
        for first, kind, side in ((0, 0, 0), (0, 0, 1), (1, 1, 0), (2, 1, 1)):
            @pl.when(i == first)
            def _():
                x2_copy(c, kind, side).start()

    def e4(c):
        for side in range(2):
            wait_through(xr2, x2t_recv, c, side)
            mine = ye2[c, (x + 1) % 4 if side == 0 else (x + 3) % 4, side]
            xr2[c, 0, side] = (mine.astype(F32) + xr2[c, 0, side].astype(F32)).astype(BF)
            x2_copy(c, 2, side).start()

    def e5(c):
        wait_tree(xr2, x2_recv, c)
        for side in range(2):
            total = ye2[c, x, side].astype(F32) + (xr2[c, 1, side].astype(F32) + xr2[c, 2, side].astype(F32))
            fin[c, :, side * HALF:(side + 1) * HALF] = total.astype(BF)
        o_copy(c).start()
        o_local(c).start()

    def e6(c):
        wait_bytes(xr2.at[c], x2_send.at[c])
        for g in range(4):
            wait_bytes(yr2.at[c * 4 + g], y2_send.at[c * 4 + g])

    def old_sends(_):
        wait_bytes(a_buf.at[1], core_send.at[0])
        wait_bytes(w_buf.at[1], core_send.at[1])
        wait_bytes(keys.at[x, pl.ds(0, 7)], key_sem.at[0])
        wait_bytes(keys.at[pl.ds(0, 3)], key_sem.at[2])

    def last_sends(_):
        for c in range(max(0, direct - slots_x), direct):
            wait_bytes(xs.at[c % slots_x, 0], xt_send.at[c])
            wait_bytes(xs.at[c % slots_x, 1], xp_send.at[c])
        for c in range(max(0, early - slots_z), early):
            for g in range(4):
                wait_z2_sent(c, g)

    plan = (
        (a0, (1, 3, 5, 7, 12)),
        (functools.partial(a1, 0), (4, 6, 17, 27, 28)),
        (functools.partial(a1, 1), (4, 6, 17, 27, 28)),
        (e0, (0, 1, 2, 5, 7, 8, 11, 13, 16, 19, 20, 23)),
        (share_keys, (0,)),
        (build, (3, 5, 7, 8)),
        (e1, (8, 9, 10, 11, 13, 18, 22, 24, 27, 28, 31, 36)),
        (e2, (11, 13, 14, 15, 19, 23, 25, 27, 28, 30, 34, 41)),
        (e3, (26, 28, 29, 35, 37, 38, 39, 40, 46, 51, 52, 54)),
        (e4, (33, 48, 52)),
        (e5, (46, 50, 55)),
        (a2, (19, 21, 23, 24, 29, 32, 36, 42, 44, 47)),
        (a3, (31, 34, 38, 42, 43, 44, 45, 47, 49, 50)),
        (a4, (36, 44, 47, 50, 51, 53, 54, 55, 56, 57)),
        (old_sends, (37,)),
        (last_sends, (51,)),
        (e6, (48, 52, 57)),
        (a5, (46, 52, 55, 57, 58)),
    )

    def step(n):
        for stage, steps in plan:
            now = [n == at for at in steps]

            @pl.when(functools.reduce(jnp.logical_or, now))
            def _():
                stage(sum(i * hit.astype(jnp.int32) for i, hit in enumerate(now)))

    loop(1 + max(max(steps) for _, steps in plan), step)
    mine = fin.at[:, pl.ds(0, TOKENS)]
    for i in range(3):
        wait_bytes(mine, o_sem.at[i])
    wait_bytes(yr.at[:, :, pl.ds(0, 2)], a_sem.at[0])


def on_device(expert_ids, hidden_grad, up_weight):
    rows, hid = hidden_grad.shape
    width = up_weight.shape[0]
    chunks = width // 2 // WIDE
    early = 3
    direct = chunks - early
    dma = pltpu.SemaphoreType.DMA
    both = 2 * TOKENS

    def vmem(*shape):
        return pltpu.VMEM(shape, BF)

    out = pl.pallas_call(
        functools.partial(kernel, direct, early),
        out_shape=pltpu.VMEM((TOKENS, width), BF),
        in_specs=[
            pl.BlockSpec(memory_space=pltpu.VMEM),
            pl.BlockSpec(memory_space=pl.ANY),
            pl.BlockSpec(memory_space=pl.ANY),
        ],
        out_specs=pl.BlockSpec(memory_space=pl.ANY),
        scratch_shapes=[
            vmem(2, rows, hid),
            vmem(2, width // 2, hid),
            vmem(3, 2, 2, GROUP, HALF),
            vmem(direct, 3, 2, GROUP, HALF),
            vmem(direct, 4, 2, BLOCK, HALF),
            vmem(direct, 2, SHARDS, TOKENS, HALF),
            vmem(2, 4, 2, GROUP, HALF),
            vmem(early, 4, 4, 2, BLOCK, HALF),
            vmem(early * 4, 2, 2, both, HALF),
            vmem(early * 4, 3, 2, both, HALF),
            vmem(early, 4, 2, both, HALF),
            vmem(early, 3, 2, both, HALF),
            vmem(4, 4, both, DEPTH),
            vmem(early, both, WIDE),
            pltpu.VMEM((4, SHARDS, 8, TOKENS), jnp.int32),
            dma((4 + chunks,)), dma((2,)), dma((4 + chunks,)), dma((4,)),
            dma((direct,)), dma((direct,)), dma((direct,)), dma((direct, 2)), dma((direct, 2)),
            dma((direct, 2)), dma((direct, 2)), dma((direct, 2)), dma((direct, 2)),
            dma((early, 4)), dma((early, 4)), dma((early * 4,)), dma((early * 4, 2)), dma((early * 4,)),
            dma((early,)), dma((early, 2)), dma((early,)), dma((3,)), dma((1,)),
        ],
        compiler_params=pltpu.CompilerParams(
            collective_id=0, has_side_effects=True, vmem_limit_bytes=61 * 2**20
        ),
        cost_estimate=pl.CostEstimate(
            flops=2 * rows * hid * width, bytes_accessed=2 * (rows + width) * hid + 2 * TOKENS * width, transcendentals=0
        ),
        name="up_cotangent",
    )(expert_ids[0].T, hidden_grad, up_weight)
    return out[None]


def solution(mesh):
    return jax.shard_map(
        on_device,
        mesh=mesh,
        in_specs=(P("dp", "expert", None), P(None, ("dp", "expert")), P(None, ("dp", "expert"))),
        out_specs=P("dp", "expert", None),
        check_vma=False,
    )
```

```python
import functools

import jax
import jax.numpy as jnp
from jax import lax
from jax.experimental import pallas as pl
from jax.experimental.pallas import tpu as pltpu
from jax.sharding import PartitionSpec as P

EXPERTS = 8
SLOTS = 34
SHARDS = 8
BLOCK = SLOTS * SHARDS
GROUP = 4 * BLOCK
WINDOW = 80
DEPTH = 4 * WINDOW
TOKENS = 128
WIDE = 256
HALF = 128
MESH = pl.DeviceIdType.MESH
BF = jnp.bfloat16
F32 = jnp.float32


def nt_dot(a, b):
    return lax.dot_general(a, b, (((1,), (1,)), ((), ())), preferred_element_type=F32)


def kernel(
    direct, early, ids_ref, hid_ref, w_ref, out_ref,
    a_buf, w_buf, xs, xr, zb, yr, zs2, zb2, ys2, yr2, ye2, xr2, sel, fin, keys,
    in_sem, core_send, core_recv, key_sem, xt_send, xp_send, xc_send, xt_recv, x_recv,
    z_send, z_recv, y_send, y_recv, z2_send, z2_recv, y2_send, y2t_recv, y2_recv, x2_send, x2t_recv, x2_recv, o_sem, a_sem,
):
    x = lax.axis_index("dp")
    col = lax.axis_index("expert")
    z, y, k = col // 8, (col // 2) % 4, col % 2
    chunks = direct + early
    half_cols = chunks * WIDE
    slots_x = xs.shape[0]
    slots_z = zs2.shape[0]

    def dev(dx=0, dz=0, dy=0, dk=0):
        return ((x + dx) % 4, ((z + dz) % 4) * 8 + ((y + dy) % 4) * 2 + (k + dk) % 2)

    def rows_of(start, size):
        return pl.ds(pl.multiple_of(start, 16), size)

    def remote(src, dst, send, recv, to):
        return pltpu.make_async_remote_copy(
            src_ref=src, dst_ref=dst, send_sem=send, recv_sem=recv, device_id=to, device_id_type=MESH
        )

    def loop(count, body):
        lax.fori_loop(0, count, lambda i, _: (body(i), 0)[1], 0)

    def nth_group(i):
        return (x + jnp.where(i < 2, i + 2, 3 - i)) % 4

    def local_a(i):
        rows = rows_of(nth_group(i) * GROUP, GROUP)
        return pltpu.make_async_copy(hid_ref.at[rows], a_buf.at[0, rows], in_sem.at[i])

    def local_w(j):
        return pltpu.make_async_copy(
            w_ref.at[rows_of(k * half_cols + j * WIDE, WIDE)], w_buf.at[0, rows_of(j * WIDE, WIDE)], in_sem.at[4 + j]
        )

    def core_a(i):
        rows = rows_of(nth_group(i) * GROUP, GROUP)
        return remote(hid_ref.at[rows], a_buf.at[1, rows], core_send.at[0], core_recv.at[i], dev(dk=1))

    def core_w(j):
        return remote(
            w_ref.at[rows_of((1 - k) * half_cols + j * WIDE, WIDE)],
            w_buf.at[1, rows_of(j * WIDE, WIDE)],
            core_send.at[1], core_recv.at[4 + j], dev(dk=1),
        )

    peers = [(dy, dk) for dy in range(4) for dk in range(2) if (dy, dk) != (0, 0)]

    def key_copy(i):
        dy, dk = peers[i]
        mine = y * 2 + k
        return remote(keys.at[x, mine], keys.at[x, mine], key_sem.at[0], key_sem.at[1], dev(dy=dy, dk=dk))

    def group_copy(i):
        return remote(keys.at[x], keys.at[x], key_sem.at[2], key_sem.at[3], dev(dx=i + 1))

    def wait_bytes(ref, sem):
        pltpu.make_async_copy(ref, ref, sem).wait()

    def tree_copy(source, recvs, s_sems, t_sem, r_sem, axis, by_side, c, kind, side):
        step = 1 if (side == 0) != (kind == 1) else -1
        src = recvs.at[c, 0, side] if kind == 2 else source(c, kind, side, step)
        return remote(
            src, recvs.at[c, kind, side], s_sems[kind].at[c // 4 if axis == "dy" else c],
            t_sem.at[c, side] if kind == 0 else r_sem.at[c, side] if by_side else r_sem.at[c], dev(**{axis: step}),
        )

    x_copy = functools.partial(
        tree_copy, lambda c, kind, side, step: xs.at[c % slots_x, kind, side], xr,
        (xt_send, xp_send, xc_send), xt_recv, x_recv, "dx", True,
    )
    def token_block(c, side, i, blocks=1):
        return xr.at[c, 2, side, rows_of(i * TOKENS, blocks * TOKENS), :]

    def y_copy(c, side, i):
        dy, dk = peers[i]
        return remote(
            token_block(c, side, (y + dy) % 4 * 2 + (k + dk) % 2), yr.at[c, side, k * 4 + y],
            y_send.at[c], y_recv.at[c, side], dev(dy=dy, dk=dk),
        )

    y2_copy = functools.partial(
        tree_copy, lambda c, kind, side, step: ys2.at[c, kind, side], yr2, (y2_send,) * 3, y2t_recv, y2_recv, "dy", False
    )
    x2_copy = functools.partial(
        tree_copy, lambda c, kind, side, step: ye2.at[c, (x + (step if kind else 2)) % 4, side], xr2,
        (x2_send,) * 3, x2t_recv, x2_recv, "dx", False,
    )

    def wait_through(recvs, t_sem, c, side):
        wait_bytes(recvs.at[c, 0, side], t_sem.at[c, side])

    def wait_tree(recvs, r_sem, c):
        wait_bytes(recvs.at[c, pl.ds(1, 2)], r_sem.at[c])

    def z_copy(c, side, dz):
        there = rows_of(((z + dz) % 4) * BLOCK, BLOCK)
        return remote(
            xr.at[c, 1, side, there, :], zb.at[c, z, side], z_send.at[c], z_recv.at[c, side], dev(dz=dz)
        )

    def z2_copy(c, g, dz):
        there = rows_of(((z + dz) % 4) * BLOCK, BLOCK)
        return remote(
            zs2.at[c % slots_z, g, :, there, :], zb2.at[c, z, g], z2_send.at[c, g], z2_recv.at[c, g], dev(dz=dz)
        )

    def wait_z2_sent(c, g):
        wait_bytes(zs2.at[c % slots_z, g, :, pl.ds(0, 3 * BLOCK), :], z2_send.at[c, g])

    def out_cols(c):
        return out_ref.at[:, pl.ds(pl.multiple_of(k * half_cols + (direct + c) * WIDE, WIDE), WIDE)]

    def o_copy(c):
        return remote(fin.at[c, rows_of((1 - k) * TOKENS, TOKENS)], out_cols(c), o_sem.at[0], o_sem.at[1], dev(dk=1))

    def o_local(c):
        return pltpu.make_async_copy(fin.at[c, rows_of(k * TOKENS, TOKENS)], out_cols(c), o_sem.at[2])

    for j in (direct, 0, 1):
        local_w(j).start()
    for i in range(4):
        local_a(i).start()
    rest = [j for j in range(2, chunks) if j != direct]
    for j in rest:
        local_w(j).start()

    barrier = pltpu.get_barrier_semaphore()
    near = [dev(dx=i) for i in (1, 2, 3)] + [dev(dz=i) for i in (1, 2, 3)] + [dev(dy=a, dk=b) for a, b in peers]
    for to in near:
        pl.semaphore_signal(barrier, inc=1, device_id=to, device_id_type=MESH)

    ids = ids_ref[...]
    experts = lax.broadcasted_iota(jnp.int32, (EXPERTS, TOKENS), 0)
    ones = [ids[i:i + 1, :] == experts for i in range(2)]
    counts = (ones[0].astype(F32) + ones[1].astype(F32)).astype(BF)
    earlier = lax.broadcasted_iota(jnp.int32, (TOKENS, TOKENS), 0) < lax.broadcasted_iota(jnp.int32, (TOKENS, TOKENS), 1)
    before = jnp.dot(counts, earlier.astype(F32).astype(BF), preferred_element_type=F32)
    code_rows = []
    for i in range(2):
        position = jnp.sum(jnp.where(ones[i], before, 0.0), axis=0, keepdims=True).astype(jnp.int32)
        if i == 1:
            position = position + (ids[0:1, :] == ids[1:2, :]).astype(jnp.int32)
        expert = ids[i:i + 1, :]
        code_rows.append((expert % 2) * DEPTH + (expert // 2) * WINDOW + position)
    row = lax.broadcasted_iota(jnp.int32, (8, TOKENS), 0)
    keys[x, y * 2 + k] = jnp.where(row == 0, code_rows[0], code_rows[1])

    pl.semaphore_wait(barrier, len(near))
    core_w(direct).start()
    core_a(0).start()
    for j in (0, 1):
        core_w(j).start()
    for i in range(7):
        key_copy(i).start()
    for i in range(1, 4):
        core_a(i).start()
    for j in rest:
        core_w(j).start()

    def product(g, c, r=0, parts=1):
        rows = rows_of(g * GROUP + r * (GROUP // parts), GROUP // parts)
        cols = rows_of(c * WIDE, WIDE)
        return nt_dot(a_buf[0, rows, :], w_buf[0, cols, :]) + nt_dot(a_buf[1, rows, :], w_buf[1, cols, :])

    def wait_a(i):
        local_a(i).wait()
        core_a(i).wait_recv()

    def wait_w(c):
        local_w(c).wait()
        core_w(c).wait_recv()

    def halves(acc):
        return [acc[:, :HALF], acc[:, HALF:]]

    def a0(c):
        wait_w(c)

        @pl.when(c >= slots_x)
        def _():
            wait_bytes(xs.at[c % slots_x, 0], xt_send.at[c - slots_x])

        for side, part in enumerate(halves(product((x + 2) % 4, c))):
            xs[c % slots_x, 0, side] = part.astype(BF)
            x_copy(c, 0, side).start()

    def a1(side, c):
        other = 1 - side

        if side == 0:
            @pl.when(c >= slots_x)
            def _():
                wait_bytes(xs.at[c % slots_x, 1], xp_send.at[c - slots_x])

        wait_through(xr, xt_recv, c, other)
        def body(r):
            part = halves(product((x + 3) % 4 if side == 0 else (x + 1) % 4, c, r, 2))
            rows = rows_of(r * (GROUP // 2), GROUP // 2)
            xr[c, 0, other, rows] = (part[other] + xr[c, 0, other, rows].astype(F32)).astype(BF)
            xs[c % slots_x, 1, side, rows] = part[side].astype(BF)

        loop(2, body)
        for kind, at in ((1, 0), (2, 1)) if side == 0 else ((2, 0), (1, 1)):
            x_copy(c, kind, at).start()

    def a2(h):
        c, side = h // 2, h % 2
        wait_bytes(xr.at[c, pl.ds(1, 2), side], x_recv.at[c, side])
        rows = rows_of(x * GROUP, GROUP)
        cols = rows_of(c * WIDE + side * HALF, HALF)
        own = nt_dot(a_buf[0, rows, :], w_buf[0, cols, :]) + nt_dot(a_buf[1, rows, :], w_buf[1, cols, :])
        total = own + (xr[c, 1, side].astype(F32) + xr[c, 2, side].astype(F32))
        xr[c, 1, side] = total.astype(BF)
        for dz in (2, 1, 3):
            z_copy(c, side, dz).start()
        zb[c, z, side] = xr[c, 1, side, rows_of(z * BLOCK, BLOCK), :]

    def to_tokens(blocks, g, yy):
        rows = rows_of(yy * 64, WINDOW)
        values = jnp.concatenate(
            [jnp.concatenate([blocks(e)[side, rows, :] for e in range(4)], axis=0) for side in range(2)], axis=1
        )
        return jnp.dot(sel[g, yy], values, preferred_element_type=F32)

    def share_keys(_):
        wait_bytes(keys.at[x, pl.ds(0, 7)], key_sem.at[1])
        for i in range(3):
            group_copy(i).start()

    def build(part):
        @pl.when(part == 0)
        def _():
            wait_bytes(keys.at[pl.ds(0, 3)], key_sem.at[3])

        lanes = lax.broadcasted_iota(jnp.int32, (TOKENS, DEPTH), 1).astype(F32)

        def body(n):
            g, yy, kk = part, n // 2, n % 2
            turned = jnp.transpose(keys[g, yy * 2 + kk].astype(F32))
            shift = (yy * 4 + kk * SLOTS - (y // 2) * DEPTH).astype(F32)
            hit = (turned[:, 0:1] + shift == lanes) | (turned[:, 1:2] + shift == lanes)
            sel[g, yy, rows_of(kk * TOKENS, TOKENS), :] = hit.astype(F32).astype(BF)

        loop(8, body)

    def a3(h):
        c, side = h // 2, h % 2
        wait_bytes(zb.at[c, pl.ds(0, 3), side], z_recv.at[c, side])

        def body(yy):
            rows = rows_of(yy * 64, WINDOW)
            values = jnp.concatenate([zb[c, e, side, rows, :] for e in range(4)], axis=0)
            acc = jnp.dot(sel[x, yy], values, preferred_element_type=F32).astype(BF)
            token_block(c, side, yy * 2, 2)[...] = acc

        loop(4, body)
        for i in (3, 4, 1, 2, 5, 6, 0):
            y_copy(c, side, i).start()
        yr[c, side, k * 4 + y] = token_block(c, side, y * 2 + k)[...]

    def a_local(c, side, core):
        cols = pl.ds(pl.multiple_of(core * half_cols + c * WIDE + side * HALF, HALF), HALF)
        return pltpu.make_async_copy(yr.at[c, side, core * 4], out_ref.at[:, cols], a_sem.at[0])

    def a4(h):
        c, side = h // 2, h % 2
        wait_bytes(yr.at[c, side, pl.ds(0, 7)], y_recv.at[c, side])
        for core in range(2):
            parts = [yr[c, side, core * 4 + i].astype(F32) for i in range(4)]
            yr[c, side, core * 4] = ((parts[0] + parts[1]) + (parts[2] + parts[3])).astype(BF)
            a_local(c, side, core).start()

    def a5(c):
        wait_bytes(xr.at[c, 0], xc_send.at[c])
        wait_bytes(xr.at[c, 2, :, pl.ds(0, 7 * TOKENS), :], y_send.at[c])
        wait_bytes(xr.at[c, 1, :, pl.ds(0, 3 * BLOCK), :], z_send.at[c])

    def e0(q):
        c, i = q // 4, q % 4
        g = nth_group(i)

        @pl.when(i == 0)
        def _():
            wait_w(direct + c)

        @pl.when(c == 0)
        def _():
            wait_a(i)

        @pl.when(c >= slots_z)
        def _():
            wait_z2_sent(c - slots_z, g)

        for side, part in enumerate(halves(product(g, direct + c))):
            zs2[c % slots_z, g, side] = part.astype(BF)
        for dz in (2, 1, 3):
            z2_copy(c, g, dz).start()
        zb2[c, z, g] = zs2[c % slots_z, g, :, rows_of(z * BLOCK, BLOCK), :]

    def e_tokens(c, g, yy):
        return to_tokens(lambda e: zb2.at[c, e, g], g, yy)

    def e1(q):
        c, g = q // 4, nth_group(q % 4)
        at = c * 4 + g
        wait_bytes(zb2.at[c, pl.ds(0, 3), g], z2_recv.at[c, g])
        for side, part in enumerate(halves(e_tokens(c, g, (y + 2) % 4))):
            ys2[at, 0, side] = part.astype(BF)
        for side in range(2):
            y2_copy(at, 0, side).start()

    def e2(q):
        c, g = q // 4, nth_group(q % 4)
        at = c * 4 + g
        for side in range(2):
            other = 1 - side
            part = halves(e_tokens(c, g, (y + 3) % 4 if side == 0 else (y + 1) % 4))
            ys2[at, 1, side] = part[side].astype(BF)
            wait_through(yr2, y2t_recv, at, other)
            yr2[at, 0, other] = (part[other] + yr2[at, 0, other].astype(F32)).astype(BF)
            y2_copy(at, 2, other).start()
            y2_copy(at, 1, side).start()

    def e3(q):
        c, i = q // 4, q % 4
        g = nth_group(i)
        at = c * 4 + g
        wait_tree(yr2, y2_recv, at)
        for side, part in enumerate(halves(e_tokens(c, g, y))):
            total = part + (yr2[at, 1, side].astype(F32) + yr2[at, 2, side].astype(F32))
            ye2[c, g, side] = total.astype(BF)
        for first, kind, side in ((0, 0, 0), (0, 0, 1), (1, 1, 0), (2, 1, 1)):
            @pl.when(i == first)
            def _():
                x2_copy(c, kind, side).start()

    def e4(c):
        for side in range(2):
            wait_through(xr2, x2t_recv, c, side)
            mine = ye2[c, (x + 1) % 4 if side == 0 else (x + 3) % 4, side]
            xr2[c, 0, side] = (mine.astype(F32) + xr2[c, 0, side].astype(F32)).astype(BF)
            x2_copy(c, 2, side).start()

    def e5(c):
        wait_tree(xr2, x2_recv, c)
        for side in range(2):
            total = ye2[c, x, side].astype(F32) + (xr2[c, 1, side].astype(F32) + xr2[c, 2, side].astype(F32))
            fin[c, :, side * HALF:(side + 1) * HALF] = total.astype(BF)
        o_copy(c).start()
        o_local(c).start()

    def e6(c):
        wait_bytes(xr2.at[c], x2_send.at[c])
        wait_bytes(yr2.at[pl.ds(c * 4, 4)], y2_send.at[c])

    def old_sends(_):
        wait_bytes(a_buf.at[1], core_send.at[0])
        wait_bytes(w_buf.at[1], core_send.at[1])
        wait_bytes(keys.at[x, pl.ds(0, 7)], key_sem.at[0])
        wait_bytes(keys.at[pl.ds(0, 3)], key_sem.at[2])

    def last_sends(_):
        for c in range(max(0, direct - slots_x), direct):
            wait_bytes(xs.at[c % slots_x, 0], xt_send.at[c])
            wait_bytes(xs.at[c % slots_x, 1], xp_send.at[c])
        for c in range(max(0, early - slots_z), early):
            for g in range(4):
                wait_z2_sent(c, g)

    plan = (
        (a0, (1, 3, 5, 7, 12)),
        (functools.partial(a1, 0), (4, 6, 17, 27, 28)),
        (functools.partial(a1, 1), (4, 6, 17, 27, 28)),
        (e0, (0, 1, 2, 5, 7, 8, 11, 13, 16, 19, 20, 23)),
        (share_keys, (0,)),
        (build, (3, 5, 7, 8)),
        (e1, (8, 9, 10, 11, 13, 18, 22, 24, 27, 28, 31, 36)),
        (e2, (11, 13, 14, 15, 19, 23, 25, 27, 28, 30, 34, 41)),
        (e3, (26, 28, 29, 35, 37, 38, 39, 40, 46, 51, 52, 54)),
        (e4, (33, 48, 52)),
        (e5, (46, 50, 55)),
        (a2, (19, 21, 23, 24, 29, 32, 36, 42, 44, 47)),
        (a3, (31, 34, 38, 42, 43, 44, 45, 47, 49, 50)),
        (a4, (36, 44, 47, 50, 51, 53, 54, 55, 56, 57)),
        (old_sends, (37,)),
        (last_sends, (51,)),
        (e6, (48, 52, 57)),
        (a5, (46, 52, 55, 57, 58)),
    )

    def step(n):
        for stage, steps in plan:
            now = [n == at for at in steps]

            @pl.when(functools.reduce(jnp.logical_or, now))
            def _():
                stage(sum(i * hit.astype(jnp.int32) for i, hit in enumerate(now)))

    loop(1 + max(max(steps) for _, steps in plan), step)
    mine = fin.at[:, pl.ds(0, TOKENS)]
    for i in range(3):
        wait_bytes(mine, o_sem.at[i])
    wait_bytes(yr.at[:, :, pl.ds(0, 2)], a_sem.at[0])


def on_device(expert_ids, hidden_grad, up_weight):
    rows, hid = hidden_grad.shape
    width = up_weight.shape[0]
    chunks = width // 2 // WIDE
    early = 3
    direct = chunks - early
    dma = pltpu.SemaphoreType.DMA
    both = 2 * TOKENS

    def vmem(*shape):
        return pltpu.VMEM(shape, BF)

    out = pl.pallas_call(
        functools.partial(kernel, direct, early),
        out_shape=pltpu.VMEM((TOKENS, width), BF),
        in_specs=[
            pl.BlockSpec(memory_space=pltpu.VMEM),
            pl.BlockSpec(memory_space=pl.ANY),
            pl.BlockSpec(memory_space=pl.ANY),
        ],
        out_specs=pl.BlockSpec(memory_space=pl.ANY),
        scratch_shapes=[
            vmem(2, rows, hid),
            vmem(2, width // 2, hid),
            vmem(3, 2, 2, GROUP, HALF),
            vmem(direct, 3, 2, GROUP, HALF),
            vmem(direct, 4, 2, BLOCK, HALF),
            vmem(direct, 2, SHARDS, TOKENS, HALF),
            vmem(2, 4, 2, GROUP, HALF),
            vmem(early, 4, 4, 2, BLOCK, HALF),
            vmem(early * 4, 2, 2, both, HALF),
            vmem(early * 4, 3, 2, both, HALF),
            vmem(early, 4, 2, both, HALF),
            vmem(early, 3, 2, both, HALF),
            vmem(4, 4, both, DEPTH),
            vmem(early, both, WIDE),
            pltpu.VMEM((4, SHARDS, 8, TOKENS), jnp.int32),
            dma((4 + chunks,)), dma((2,)), dma((4 + chunks,)), dma((4,)),
            dma((direct,)), dma((direct,)), dma((direct,)), dma((direct, 2)), dma((direct, 2)),
            dma((direct,)), dma((direct, 2)), dma((direct,)), dma((direct, 2)),
            dma((early, 4)), dma((early, 4)), dma((early,)), dma((early * 4, 2)), dma((early * 4,)),
            dma((early,)), dma((early, 2)), dma((early,)), dma((3,)), dma((1,)),
        ],
        compiler_params=pltpu.CompilerParams(
            collective_id=0, has_side_effects=True, vmem_limit_bytes=61 * 2**20
        ),
        cost_estimate=pl.CostEstimate(
            flops=2 * rows * hid * width, bytes_accessed=2 * (rows + width) * hid + 2 * TOKENS * width, transcendentals=0
        ),
        name="up_cotangent",
    )(expert_ids[0].T, hidden_grad, up_weight)
    return out[None]


def solution(mesh):
    return jax.shard_map(
        on_device,
        mesh=mesh,
        in_specs=(P("dp", "expert", None), P(None, ("dp", "expert")), P(None, ("dp", "expert"))),
        out_specs=P("dp", "expert", None),
        check_vma=False,
    )
```
